128 devices in a mesh: row: 16 (over y_lo, z, core), col: 8 (over x, y_hi).
Axes of the slice: x: 4, y: 4 (y_hi: 2, y_lo: 2; y = y_hi * 2 + y_lo), z: 4, core: 2. Of those that a mesh axis runs over, the one named last changes fastest.
Arguments:
- tokens: bfloat16 [2048, 6144], P('row', 'col'), may hold values from -8 to 8
- cotangent: bfloat16 [2048, 6144], P('row', 'col'), may hold values from -6 to 6
- w_in: bfloat16 [6144, 12288], P('col', 'row'), may hold values from -0.078125 to 0.078125
- w_out: bfloat16 [12288, 6144], P('row', 'col'), may hold values from -0.18042196 to 0.18042196
- first_moment: float32 [6144, 12288], P('col', 'row'), may hold values from -0.6 to 0.6
- rotated_second_moment: float32 [6144, 12288], P('col', 'row'), may hold values from 0.01 to 0.05
- left_basis: float32 [6144, 768], P('col'), may hold values from -2 to 2
- right_basis: float32 [12288, 768], P('row'), may hold values from -2 to 2
Outputs:
- layer_out: bfloat16 [2048, 6144], P('row', 'col')
- input_grad: bfloat16 [2048, 6144], P('row', 'col')
- out_grad: bfloat16 [12288, 6144], P('row', 'col')
- update: float32 [6144, 12288], P('col', 'row')
- new_first: float32 [6144, 12288], P('col', 'row')
- new_second: float32 [6144, 12288], P('col', 'row')
- left_stat: float32 [6144, 768], P(('col', 'row'))
- right_stat: float32 [12288, 768], P(('row', 'col'))
The draws below stay inside these ranges and needn't reach their ends.
All inputs are finite; a program needn't handle non-finite values.
Results may differ from the reference program's by a relative error of at most 0.022.
Values may be sent and summed in bfloat16 or wider, within the bound.
No kernel may reach another device: no remote copies, remote signals or barrier semaphores. Data moves between devices by JAX's collectives and lax.ppermute only.
A program may use at most 128 MiB of HBM per device.

```python
import math
import jax
import jax.numpy as jnp
from jax import lax

D = 6144
HID = 12288
TOKENS = 2048
DBL = 768
HBL = 768
N_ROW = 16
N_COL = 8


def draw_tokens(key, part):
    key = jax.random.fold_in(key, 11)
    subkeys = jax.random.split(key, 2)
    position = jnp.arange(D, dtype=jnp.float32) / (D - 1)
    ramp_up = jnp.exp(position * 1.0986122886681098)
    spread = jax.random.uniform(subkeys[0], (D,), jnp.float32, -1.15, 1.15)
    values = jax.random.normal(subkeys[1], (TOKENS, D), jnp.float32)
    column = ramp_up * jnp.exp(spread) * 0.358
    return jnp.clip(values * column[None, :], -8.0, 8.0).astype(jnp.bfloat16)


def draw_w_out(key, part):
    key = jax.random.fold_in(key, 23)
    subkeys = jax.random.split(key, 2)
    position = jnp.arange(HID, dtype=jnp.float32) / (HID - 1)
    ramp_up = jnp.exp(position * 1.0986122886681098)
    spread = jax.random.uniform(subkeys[0], (HID,), jnp.float32, -1.15, 1.15)
    entries = jnp.clip(jax.random.normal(subkeys[1], (HID, D), jnp.float32), -6.0, 6.0)
    row_scale = ramp_up * jnp.exp(spread) * 0.358 * HID ** (-0.5)
    limit = 20.0 * HID ** (-0.5)
    return jnp.clip(entries * row_scale[:, None], -limit, limit).astype(jnp.bfloat16)


def draw_left_basis(key, part):
    key = jax.random.fold_in(key, 37)
    row_index = jnp.arange(D, dtype=jnp.int32)[:, None] % DBL
    col_index = jnp.arange(DBL, dtype=jnp.int32)[None, :]
    identity = jnp.where(row_index == col_index, 1.0, 0.0).astype(jnp.float32)
    noise = jnp.clip(jax.random.normal(key, (D, DBL), jnp.float32), -4.0, 4.0)
    return jnp.clip(identity + 0.6 * noise * DBL ** (-0.5), -2.0, 2.0)


def draw_right_basis(key, part):
    key = jax.random.fold_in(key, 41)
    row_index = jnp.arange(HID, dtype=jnp.int32)[:, None] % HBL
    col_index = jnp.arange(HBL, dtype=jnp.int32)[None, :]
    identity = jnp.where(row_index == col_index, 1.0, 0.0).astype(jnp.float32)
    noise = jnp.clip(jax.random.normal(key, (HID, HBL), jnp.float32), -4.0, 4.0)
    return jnp.clip(identity + 0.6 * noise * HBL ** (-0.5), -2.0, 2.0)


def steps_of(own_key, shape, pieces, smallest, high):
    level = 1.0
    for axis_at, parts in pieces:
        draws = jax.random.uniform(jax.random.fold_in(jax.random.fold_in(own_key, 6), axis_at), (parts,), jnp.float32, smallest / len(pieces), high / len(pieces))
        level = level * jnp.repeat(jnp.exp(draws), shape[axis_at] // parts).reshape((-1,) + (1,) * (len(shape) - 1 - axis_at))
    return level


def bell_draw(rng, dims, deviation, bound, shards=(), kind=jnp.bfloat16):
    result = jax.random.normal(rng, dims, jnp.float32) * deviation
    if len(shards) > 0:
        result = steps_of(rng, dims, shards, -0.22, 0.18) * result
    return jnp.clip(result, min=-bound, max=bound).astype(kind)


def setup_inputs(seed: int = 0) -> dict:
    streams_of = jax.random.split(jax.random.key(seed), 9)
    tokens = draw_tokens(jax.random.fold_in(streams_of[8], 71), 0)
    cotangent = bell_draw(streams_of[1], (TOKENS, D), 1.0, 6.0, ((0, 16), (1, 8)))
    w_in = bell_draw(streams_of[2], (D, HID), D ** -0.5, 0.078125, ((0, 8), (1, 16)))
    w_out = draw_w_out(jax.random.fold_in(streams_of[8], 71), 0)
    first_moment = bell_draw(streams_of[4], (D, HID), 0.1, 0.6, ((0, 8), (1, 16)), jnp.float32)
    rotated_second_moment = jnp.clip(jnp.exp(math.log(0.05) - 1.609438 * jax.random.uniform(streams_of[5], (D, HID), jnp.float32) ** steps_of(streams_of[5], (D, HID), ((0, 8), (1, 16)), -0.2, 0.2)), 0.01, 0.05)
    left_basis = draw_left_basis(jax.random.fold_in(streams_of[8], 71), 0)
    right_basis = draw_right_basis(jax.random.fold_in(streams_of[8], 71), 0)
    return {"tokens": tokens, "cotangent": cotangent, "w_in": w_in, "w_out": w_out, "first_moment": first_moment, "rotated_second_moment": rotated_second_moment, "left_basis": left_basis, "right_basis": right_basis}


exact_precision = lax.Precision.HIGHEST
contract_last = (((1,), (1,)), ((), ()))
contract_first = (((0,), (0,)), ((), ()))

def gelu_pair(hidden):
    normal_cdf = 0.5 * (1.0 + jax.scipy.special.erf(hidden * 0.7071067811865476))
    activation = hidden * normal_cdf
    derivative = normal_cdf + hidden * jnp.exp(-0.5 * hidden * hidden) * 0.3989422804014327
    return (activation, derivative)

def reference(tokens, cotangent, w_in, w_out, first_moment, rotated_second_moment, left_basis, right_basis):
    grad_scale = TOKENS ** (-0.5)
    hidden = jnp.dot(tokens, w_in, preferred_element_type=jnp.float32)
    back = lax.dot_general(cotangent, w_out, contract_last, preferred_element_type=jnp.float32)
    activation, derivative = gelu_pair(hidden)
    act = activation.astype(jnp.bfloat16)
    grad_hidden = (back * derivative).astype(jnp.bfloat16)
    out_total = jnp.zeros((TOKENS, D), jnp.float32)
    grad_total = jnp.zeros((TOKENS, D), jnp.float32)
    for block in range(N_ROW):
        lower = block * HBL
        act_block = act[:, lower:lower + HBL]
        grad_block = grad_hidden[:, lower:lower + HBL]
        out_part = jnp.dot(act_block, w_out[lower:lower + HBL, :], preferred_element_type=jnp.float32)
        grad_part = lax.dot_general(grad_block, w_in[:, lower:lower + HBL], contract_last, preferred_element_type=jnp.float32)
        out_total = out_total + out_part.astype(jnp.bfloat16).astype(jnp.float32)
        grad_total = grad_total + grad_part.astype(jnp.bfloat16).astype(jnp.float32)
    layer_out = out_total.astype(jnp.bfloat16)
    input_grad = grad_total.astype(jnp.bfloat16)
    out_grad = (grad_scale * lax.dot_general(act, cotangent, contract_first, preferred_element_type=jnp.float32)).astype(jnp.bfloat16)
    weight_grad = grad_scale * lax.dot_general(tokens, grad_hidden, contract_first, preferred_element_type=jnp.float32)
    by_rows = weight_grad.reshape(N_COL, DBL, HID)
    left_stat = (jnp.einsum('jah,jbh->jab', by_rows, by_rows, precision=exact_precision) / HID).reshape(D, DBL)
    by_cols = weight_grad.reshape(D, N_ROW, HBL)
    right_stat = (jnp.einsum('dic,die->ice', by_cols, by_cols, precision=exact_precision) / D).reshape(HID, HBL)
    tiles = weight_grad.reshape(N_COL, DBL, N_ROW, HBL)
    left_blocks = left_basis.reshape(N_COL, DBL, DBL)
    right_block_list = right_basis.reshape(N_ROW, HBL, HBL)
    left_rotation = jnp.einsum('jba,jbic->jaic', left_blocks, tiles, precision=exact_precision)
    rotated_gradient = jnp.einsum('bgwx,wxl->bgwl', left_rotation, right_block_list, precision=exact_precision)
    moment_one = first_moment.reshape(N_COL, DBL, N_ROW, HBL)
    moment_two = rotated_second_moment.reshape(N_COL, DBL, N_ROW, HBL)
    new_first = 0.9 * moment_one + 0.1 * rotated_gradient
    new_second = 0.95 * moment_two + 0.05 * rotated_gradient * rotated_gradient
    ratio = new_first / (jnp.sqrt(new_second) + 1e-08)
    backward_left_factor = jnp.einsum('jab,jbic->jaic', left_blocks, ratio, precision=exact_precision)
    update = jnp.einsum('jaie,ice->jaic', backward_left_factor, right_block_list, precision=exact_precision)
    return (layer_out, input_grad, out_grad, update.reshape(D, HID), new_first.reshape(D, HID), new_second.reshape(D, HID), left_stat, right_stat)
```

```python
import jax
import jax.numpy as jnp
from jax import lax
from jax.sharding import Mesh, PartitionSpec as P

D = 6144
HID = 12288

bf16 = jnp.bfloat16
f32 = jnp.float32

ROW = ("yl", "z", "c")
COL = ("x", "yh")
SIZES = {"yl": 2, "z": 4, "c": 2, "x": 4, "yh": 2}


def gelu_pair(hidden):
    normal_cdf = 0.5 * (1.0 + jax.scipy.special.erf(hidden * 0.7071067811865476))
    activation = hidden * normal_cdf
    derivative = normal_cdf + hidden * jnp.exp(-0.5 * hidden * hidden) * 0.3989422804014327
    return (activation, derivative)


def dot(a, b, ca, cb):
    return lax.dot_general(
        a.astype(bf16), b.astype(bf16), (((ca,), (cb,)), ((), ())), preferred_element_type=f32
    )


def shift(value, axis, by):
    size = SIZES[axis]
    return lax.ppermute(value, axis, [(i, (i + by) % size) for i in range(size)])


def pick(blocks, index):
    return lax.dynamic_index_in_dim(blocks, index, 0, keepdims=False)


def add(*terms):
    total = terms[0].astype(f32)
    for term in terms[1:]:
        total = total + term.astype(f32)
    return total


def scatter_pair(halves, axis):
    me = lax.axis_index(axis)
    first, second = halves
    mine = jnp.where(me == 0, first, second)
    other = jnp.where(me == 0, second, first).astype(bf16)
    return add(mine, shift(other, axis, 1))


def scatter_ring(parts, ring, pair):
    far_a = shift(parts[2][0], ring, 1)
    far_b = shift(parts[2][1], ring, -1)
    near_b = shift(parts[1][1], ring, 1)
    near_a = shift(parts[3][0], ring, -1)
    sum_a = shift(add(parts[1][0], far_a).astype(bf16), ring, 1)
    sum_b = shift(add(parts[3][1], far_b).astype(bf16), ring, -1)
    return scatter_pair((add(parts[0][0], sum_a, near_a), add(parts[0][1], near_b, sum_b)), pair)


def scatter_col(value):
    blocks = value.reshape(4, 2, value.shape[0] // 8, value.shape[1])
    x = lax.axis_index("x")
    return scatter_ring([pick(blocks, (x + k) % 4) for k in range(4)], "x", "yh")


def scatter_row(value):
    blocks = value.reshape(2, 4, 2, value.shape[0] // 16, value.shape[1])
    core, z = lax.axis_index("c"), lax.axis_index("z")
    mine = lax.dynamic_index_in_dim(blocks, core, 2, keepdims=False)
    other = lax.dynamic_index_in_dim(blocks, 1 - core, 2, keepdims=False)
    chip = add(mine, shift(other, "c", 1)).astype(bf16)
    parts = [lax.dynamic_index_in_dim(chip, (z + k) % 4, 1, keepdims=False) for k in range(4)]
    return scatter_ring(parts, "z", "yl")


def gather_col(block):
    x, yh = lax.axis_index("x"), lax.axis_index("yh")
    rows = block.shape[0]
    pair = shift(block, "yh", 1)
    left, right = shift(block, "x", 1), shift(block, "x", -1)
    far = shift(left, "x", 1)
    pair_left, pair_right = shift(pair, "x", 1), shift(pair, "x", -1)
    pair_far = shift(pair_right, "x", -1)
    whole = jnp.zeros((8 * rows,) + block.shape[1:], block.dtype)
    for by, mine, others in ((0, block, pair), (3, left, pair_left), (2, far, pair_far), (1, right, pair_right)):
        base = ((x + by) % 4) * 2
        whole = lax.dynamic_update_slice_in_dim(whole, mine, (base + yh) * rows, 0)
        whole = lax.dynamic_update_slice_in_dim(whole, others, (base + 1 - yh) * rows, 0)
    return whole


def hidden_terms(all_rows, weight, contract):
    x = lax.axis_index("x")
    blocks = all_rows.reshape(4, all_rows.shape[0] // 4, all_rows.shape[1])
    parts = [None] * 4
    for k in (2, 1, 3, 0):
        part = dot(pick(blocks, (x + k) % 4), weight, 1, contract).astype(bf16)
        parts[k] = part.reshape(2, part.shape[0] // 2, part.shape[1])
    return parts


def shards(
    tokens, cotangent, w_in, w_out, first_moment, rotated_second_moment, left_basis, right_basis
):
    token_all = lax.all_gather(tokens, ROW, axis=0, tiled=True)
    token_all, cotangent = lax.optimization_barrier((token_all, cotangent))
    cot_all = lax.all_gather(cotangent, ROW, axis=0, tiled=True)
    token_count = token_all.shape[0]
    grad_scale = token_count ** (-0.5)

    forward = scatter_ring(hidden_terms(token_all, w_in, 0), "x", "yh")
    activation, derivative = gelu_pair(forward)
    act_all = gather_col(activation.astype(bf16))
    backward = scatter_ring(hidden_terms(cot_all, w_out, 1), "x", "yh")
    grad_all = gather_col((backward * derivative).astype(bf16))

    layer_out = scatter_row(dot(act_all, w_out, 1, 0).astype(bf16)).astype(bf16)
    out_grad = (grad_scale * dot(act_all, cot_all, 0, 0)).astype(bf16)
    input_grad = scatter_row(dot(grad_all, w_in, 1, 1).astype(bf16)).astype(bf16)
    weight_grad = (grad_scale * dot(token_all, grad_all, 0, 0)).astype(bf16)
    left_stat = scatter_row((dot(weight_grad, weight_grad, 1, 1) / HID).astype(bf16))
    right_stat = scatter_col((dot(weight_grad, weight_grad, 0, 0) / D).astype(bf16))

    rotated = dot(dot(left_basis, weight_grad, 0, 0), right_basis, 1, 0)
    new_first = 0.9 * first_moment + 0.1 * rotated
    new_second = 0.95 * rotated_second_moment + 0.05 * rotated * rotated
    ratio = new_first / (jnp.sqrt(new_second) + 1e-08)
    update = dot(dot(left_basis, ratio, 1, 0), right_basis, 1, 1)
    return (layer_out, input_grad, out_grad, update, new_first, new_second, left_stat, right_stat)


def solution(mesh):
    fine = Mesh(mesh.devices.reshape(2, 4, 2, 4, 2), ROW + COL)
    in_specs = (
        P(ROW, COL),
        P(ROW, COL),
        P(COL, ROW),
        P(ROW, COL),
        P(COL, ROW),
        P(COL, ROW),
        P(COL, None),
        P(ROW, None),
    )
    out_specs = (
        P(ROW, COL),
        P(ROW, COL),
        P(ROW, COL),
        P(COL, ROW),
        P(COL, ROW),
        P(COL, ROW),
        P(COL + ROW, None),
        P(ROW + COL, None),
    )
    return jax.shard_map(shards, mesh=fine, in_specs=in_specs, out_specs=out_specs, check_vma=False)
```

```python
import jax
import jax.numpy as jnp
from jax import lax
from jax.sharding import Mesh, PartitionSpec as P

D = 6144
HID = 12288

bf16 = jnp.bfloat16
f32 = jnp.float32

ROW = ("yl", "z", "c")
COL = ("x", "yh")
SIZES = {"yl": 2, "z": 4, "c": 2, "x": 4, "yh": 2}


def gelu_pair(hidden):
    normal_cdf = 0.5 * (1.0 + jax.scipy.special.erf(hidden * 0.7071067811865476))
    activation = hidden * normal_cdf
    derivative = normal_cdf + hidden * jnp.exp(-0.5 * hidden * hidden) * 0.3989422804014327
    return (activation, derivative)


def dot(a, b, ca, cb):
    return lax.dot_general(
        a.astype(bf16), b.astype(bf16), (((ca,), (cb,)), ((), ())), preferred_element_type=f32
    )


def shift(value, axis, by):
    size = SIZES[axis]
    return lax.ppermute(value, axis, [(i, (i + by) % size) for i in range(size)])


def add(*terms):
    total = terms[0].astype(f32)
    for term in terms[1:]:
        total = total + term.astype(f32)
    return total


def along(blocks, index, axis=0):
    return lax.dynamic_index_in_dim(blocks, index, axis, keepdims=False)


def swap_halves(first, second, index, axis):
    mine = jnp.where(index == 0, first, second)
    other = jnp.where(index == 0, second, first).astype(bf16)
    return add(mine, shift(other, axis, 1))


def ring_sum(parts, ring):
    arrived = [shift(parts[k].astype(bf16), ring, k) for k in (2, 1, 3)]
    return add(parts[0], *arrived)


def chip_sum(value, core, axis):
    other = along(value, 1 - core, axis)
    return add(along(value, core, axis), shift(other, "c", 1)).astype(bf16)


def ring_gather(block):
    return jnp.stack([block] + [shift(block, "x", -k) for k in (1, 2, 3)])


def shards(
    tokens, cotangent, w_in, w_out, first_moment, rotated_second_moment, left_basis, right_basis
):
    yl, z, c, x, yh = (lax.axis_index(name) for name in ROW + COL)
    both = lax.all_gather(jnp.stack([tokens, cotangent]), ROW, axis=1, tiled=True)
    token_all, cot_all = both[0], both[1]
    token_count, width = token_all.shape
    rows = token_count // 8
    grad_scale = token_count ** (-0.5)
    token_blocks = token_all.reshape(2, 4, rows, width)
    cot_blocks = cot_all.reshape(2, 4, rows, width)

    parts = [None] * 4
    for k in (2, 1, 3, 0):
        parts[k] = dot(along(token_blocks, (x + k) % 4, 1), w_in, 2, 0)
    total = ring_sum(parts, "x")
    forward = swap_halves(total[0], total[1], yh, "yh")

    leaving = dot(along(cot_blocks, 1 - yh), w_out, 2, 1).astype(bf16)
    staying = dot(along(cot_blocks, yh), w_out, 2, 1)
    total = add(staying, shift(leaving, "yh", 1))
    backward = ring_sum([along(total, (x + k) % 4) for k in range(4)], "x")

    activation, derivative = gelu_pair(forward)
    act = activation.astype(bf16)
    grad = (backward * derivative).astype(bf16)

    act_own = ring_gather(act)
    act_other = shift(act_own, "yh", 1)
    grad_own = ring_gather(grad)
    grad_other = ring_gather(shift(grad, "yh", 1))

    def turned(blocks):
        doubled = jnp.concatenate([blocks, blocks], axis=1)
        ring = lax.dynamic_slice_in_dim(doubled, x, 4, 1)
        return along(ring, yh), along(ring, 1 - yh)

    token_own, token_other = turned(token_blocks)
    cot_own, cot_other = turned(cot_blocks)

    def flat(value):
        return value.reshape(-1, value.shape[-1])

    def along_z(value):
        cores = chip_sum(value.reshape(4, 2, rows // 2, width), c, 1)
        return ring_sum([along(cores, (z - x + j) % 4) for j in range(4)], "z")

    def token_sum(own, other):
        mine = along_z(dot_bf(own[0], own[1], own[2]))
        theirs = along_z(dot_bf(other[0], other[1], other[2]))
        return swap_halves(mine, theirs, yl ^ yh, "yl").astype(bf16)

    def dot_bf(value, weight, contract):
        return dot(value, weight, 2, contract).astype(bf16)

    layer_out = token_sum((act_own, w_out, 0), (act_other, w_out, 0))
    input_grad = token_sum((grad_own, w_in, 1), (grad_other, w_in, 1))

    out_grad = (
        grad_scale
        * (dot(flat(act_own), flat(cot_own), 0, 0) + dot(flat(act_other), flat(cot_other), 0, 0))
    ).astype(bf16)
    weight_grad = grad_scale * (
        dot(flat(token_own), flat(grad_own), 0, 0) + dot(flat(token_other), flat(grad_other), 0, 0)
    )
    rounded_grad = weight_grad.astype(bf16)

    left = (dot(rounded_grad, rounded_grad, 1, 1) / HID).astype(bf16)
    cores = chip_sum(left.reshape(2, 4, 2, left.shape[0] // 16, left.shape[1]), c, 2)
    pair = ring_sum([along(cores, (z + j) % 4, 1) for j in range(4)], "z")
    left_stat = swap_halves(pair[0], pair[1], yl, "yl")

    right = (dot(rounded_grad, rounded_grad, 0, 0) / D).astype(bf16)
    blocks = right.reshape(4, 2, right.shape[0] // 8, right.shape[1])
    pair = ring_sum([along(blocks, (x + k) % 4) for k in range(4)], "x")
    right_stat = swap_halves(pair[0], pair[1], yh, "yh")

    def fine_dot(a, b, ca, cb):
        return lax.dot_general(
            a, b, (((ca,), (cb,)), ((), ())), precision=lax.Precision.HIGH, preferred_element_type=f32
        )

    rotated = fine_dot(fine_dot(left_basis, weight_grad, 0, 0), right_basis, 1, 0)
    new_first = 0.9 * first_moment + 0.1 * rotated
    new_second = 0.95 * rotated_second_moment + 0.05 * rotated * rotated
    ratio = new_first / (jnp.sqrt(new_second) + 1e-08)
    update = dot(dot(left_basis, ratio, 1, 0), right_basis, 1, 1)
    return (layer_out, input_grad, out_grad, update, new_first, new_second, left_stat, right_stat)


def solution(mesh):
    fine = Mesh(mesh.devices.reshape(2, 4, 2, 4, 2), ROW + COL)
    in_specs = (
        P(ROW, COL),
        P(ROW, COL),
        P(COL, ROW),
        P(ROW, COL),
        P(COL, ROW),
        P(COL, ROW),
        P(COL, None),
        P(ROW, None),
    )
    out_specs = (
        P(ROW, COL),
        P(ROW, COL),
        P(ROW, COL),
        P(COL, ROW),
        P(COL, ROW),
        P(COL, ROW),
        P(COL + ROW, None),
        P(ROW + COL, None),
    )
    return jax.shard_map(shards, mesh=fine, in_specs=in_specs, out_specs=out_specs, check_vma=False)
```

```python
import jax
import jax.numpy as jnp
from jax import lax
from jax.sharding import Mesh, PartitionSpec as P

D = 6144
HID = 12288

bf16 = jnp.bfloat16
f32 = jnp.float32

ROW = ("yl", "z", "c")
COL = ("x", "yh")
SIZES = {"yl": 2, "z": 4, "c": 2, "x": 4, "yh": 2}


def gelu_pair(hidden):
    normal_cdf = 0.5 * (1.0 + jax.scipy.special.erf(hidden * 0.7071067811865476))
    activation = hidden * normal_cdf
    derivative = normal_cdf + hidden * jnp.exp(-0.5 * hidden * hidden) * 0.3989422804014327
    return (activation, derivative)


def dot(a, b, ca, cb):
    return lax.dot_general(
        a.astype(bf16), b.astype(bf16), (((ca,), (cb,)), ((), ())), preferred_element_type=f32
    )


def shift(value, axis, by):
    size = SIZES[axis]
    return lax.ppermute(value, axis, [(i, (i + by) % size) for i in range(size)])


def add(*terms):
    total = terms[0].astype(f32)
    for term in terms[1:]:
        total = total + term.astype(f32)
    return total


def along(blocks, index, axis=0):
    return lax.dynamic_index_in_dim(blocks, index, axis, keepdims=False)


def swap_halves(first, second, index, axis):
    mine = jnp.where(index == 0, first, second)
    other = jnp.where(index == 0, second, first).astype(bf16)
    return add(mine, shift(other, axis, 1))


def ring_send(parts, ring):
    return [shift(parts[k].astype(bf16), ring, k) for k in (2, 1, 3)]


def chip_sum(value, core, axis):
    other = along(value, 1 - core, axis)
    return add(along(value, core, axis), shift(other, "c", 1)).astype(bf16)


def ring_gather(block):
    return [shift(block, "x", -k) for k in (1, 2, 3)]


def shards(
    tokens, cotangent, w_in, w_out, first_moment, rotated_second_moment, left_basis, right_basis
):
    yl, z, c, x, yh = (lax.axis_index(name) for name in ROW + COL)
    both = lax.all_gather(jnp.stack([tokens, cotangent]), ROW, axis=1, tiled=True)
    token_all, cot_all = both[0], both[1]
    token_count, width = token_all.shape
    rows = token_count // 8
    grad_scale = token_count ** (-0.5)
    token_blocks = token_all.reshape(2, 4, rows, width)
    cot_blocks = cot_all.reshape(2, 4, rows, width)

    def turned(blocks):
        doubled = jnp.concatenate([blocks, blocks], axis=1)
        ring = lax.dynamic_slice_in_dim(doubled, x, 4, 1)
        return along(ring, yh), along(ring, 1 - yh)

    def flat(value):
        return value.reshape(-1, value.shape[-1])

    def cores_sum(value):
        return chip_sum(value.reshape(4, 2, rows // 2, width), c, 1)

    def by_z(cores):
        return [along(cores, (z - x + j) % 4) for j in range(4)]

    leaving = dot(along(cot_blocks, 1 - yh), w_out, 2, 1).astype(bf16)
    parts = [None] * 4
    for k in (2, 1, 3):
        parts[k] = dot(along(token_blocks, (x + k) % 4, 1), w_in, 2, 0).astype(bf16)
    arrived_back = shift(leaving, "yh", 1)
    arrived = ring_send(parts, "x")
    parts[0] = dot(along(token_blocks, x, 1), w_in, 2, 0)
    staying = dot(along(cot_blocks, yh), w_out, 2, 1)
    token_own, token_other = turned(token_blocks)
    cot_own, cot_other = turned(cot_blocks)
    arrived, arrived_back, kept, staying, token_own, token_other, cot_own, cot_other = lax.optimization_barrier(
        (arrived, arrived_back, parts[0], staying, token_own, token_other, cot_own, cot_other)
    )

    total_back = add(staying, arrived_back)
    parts = [along(total_back, (x + k) % 4) for k in range(4)]
    arrived_back = ring_send(parts, "x")
    total = add(kept, *arrived)
    forward = swap_halves(total[0], total[1], yh, "yh")
    activation, derivative = gelu_pair(forward)
    act = activation.astype(bf16)
    arrived_back, act, derivative = lax.optimization_barrier((arrived_back, act, derivative))

    act_ring = ring_gather(act)
    grad = (add(parts[0], *arrived_back) * derivative).astype(bf16)
    pair = shift(grad, "yh", 1)
    act_ring, grad, pair = lax.optimization_barrier((act_ring, grad, pair))

    act_own = jnp.stack([act] + act_ring)
    near = shift(act_own[:2], "yh", 1)
    grad_ring = ring_gather(grad)
    mixed_own = cores_sum(dot(act_own, w_out, 2, 0).astype(bf16))
    out_grad = dot(flat(act_own), flat(cot_own), 0, 0)
    near, grad_ring, mixed_own, out_grad, pair = lax.optimization_barrier(
        (near, grad_ring, mixed_own, out_grad, pair)
    )

    far = shift(act_own[2:], "yh", 1)
    pair_ring = ring_gather(pair)
    mixed_parts = by_z(mixed_own)
    mixed_arrived = ring_send(mixed_parts, "z")
    grad_own = jnp.stack([grad] + grad_ring)
    carried_own = cores_sum(dot(grad_own, w_in, 2, 1).astype(bf16))
    weight_grad = dot(flat(token_own), flat(grad_own), 0, 0)
    far, pair_ring, mixed_arrived, carried_own, weight_grad = lax.optimization_barrier(
        (far, pair_ring, mixed_arrived, carried_own, weight_grad)
    )

    carried_parts = by_z(carried_own)
    carried_arrived = ring_send(carried_parts, "z")
    grad_other = jnp.stack([pair] + pair_ring)
    act_other = jnp.concatenate([near, far])
    carried_other = cores_sum(dot(grad_other, w_in, 2, 1).astype(bf16))
    mixed_other = cores_sum(dot(act_other, w_out, 2, 0).astype(bf16))
    weight_grad = grad_scale * (weight_grad + dot(flat(token_other), flat(grad_other), 0, 0))
    rounded_grad = weight_grad.astype(bf16)
    right = (dot(rounded_grad, rounded_grad, 0, 0) / D).astype(bf16)
    left = (dot(rounded_grad, rounded_grad, 1, 1) / HID).astype(bf16)
    left = chip_sum(left.reshape(2, 4, 2, left.shape[0] // 16, left.shape[1]), c, 2)
    carried_arrived, carried_other, mixed_other, weight_grad, right, left = lax.optimization_barrier(
        (carried_arrived, carried_other, mixed_other, weight_grad, right, left)
    )

    other_parts = [jnp.stack(both) for both in zip(by_z(mixed_other), by_z(carried_other))]
    other_arrived = ring_send(other_parts, "z")
    left_parts = [along(left, (z + j) % 4, 1) for j in range(4)]
    left_arrived = ring_send(left_parts, "z")
    blocks = right.reshape(4, 2, right.shape[0] // 8, right.shape[1])
    right_parts = [along(blocks, (x + k) % 4) for k in range(4)]
    right_arrived = ring_send(right_parts, "x")

    def fine_dot(a, b, ca, cb):
        return lax.dot_general(
            a, b, (((ca,), (cb,)), ((), ())), precision=lax.Precision.HIGH, preferred_element_type=f32
        )

    rotated = fine_dot(fine_dot(left_basis, weight_grad, 0, 0), right_basis, 1, 0)
    new_first = 0.9 * first_moment + 0.1 * rotated
    new_second = 0.95 * rotated_second_moment + 0.05 * rotated * rotated
    ratio = new_first / (jnp.sqrt(new_second) + 1e-08)
    out_grad = (grad_scale * (out_grad + dot(flat(act_other), flat(cot_other), 0, 0))).astype(bf16)
    other_arrived, left_arrived, right_arrived, new_first, new_second, ratio = lax.optimization_barrier(
        (other_arrived, left_arrived, right_arrived, new_first, new_second, ratio)
    )

    mine = jnp.stack([add(mixed_parts[0], *mixed_arrived), add(carried_parts[0], *carried_arrived)])
    theirs = add(other_parts[0], *other_arrived)
    tokens_sum = swap_halves(mine, theirs, yl ^ yh, "yl").astype(bf16)
    layer_out, input_grad = tokens_sum[0], tokens_sum[1]
    left = add(left_parts[0], *left_arrived)
    left_stat = swap_halves(left[0], left[1], yl, "yl")
    right = add(right_parts[0], *right_arrived)
    right_stat = swap_halves(right[0], right[1], yh, "yh")
    update = dot(dot(left_basis, ratio, 1, 0), right_basis, 1, 1)
    return (layer_out, input_grad, out_grad, update, new_first, new_second, left_stat, right_stat)


def solution(mesh):
    fine = Mesh(mesh.devices.reshape(2, 4, 2, 4, 2), ROW + COL)
    in_specs = (
        P(ROW, COL),
        P(ROW, COL),
        P(COL, ROW),
        P(ROW, COL),
        P(COL, ROW),
        P(COL, ROW),
        P(COL, None),
        P(ROW, None),
    )
    out_specs = (
        P(ROW, COL),
        P(ROW, COL),
        P(ROW, COL),
        P(COL, ROW),
        P(COL, ROW),
        P(COL, ROW),
        P(COL + ROW, None),
        P(ROW + COL, None),
    )
    return jax.shard_map(shards, mesh=fine, in_specs=in_specs, out_specs=out_specs, check_vma=False)
```

```python
import jax
import jax.numpy as jnp
from jax import lax
from jax.sharding import Mesh, PartitionSpec as P

D = 6144
HID = 12288

bf16 = jnp.bfloat16
f32 = jnp.float32

ROW = ("yl", "z", "c")
COL = ("x", "yh")
SIZES = {"yl": 2, "z": 4, "c": 2, "x": 4, "yh": 2}


def gelu_pair(hidden):
    normal_cdf = 0.5 * (1.0 + jax.scipy.special.erf(hidden * 0.7071067811865476))
    activation = hidden * normal_cdf
    derivative = normal_cdf + hidden * jnp.exp(-0.5 * hidden * hidden) * 0.3989422804014327
    return (activation, derivative)


def dot(a, b, ca, cb):
    return lax.dot_general(
        a.astype(bf16), b.astype(bf16), (((ca,), (cb,)), ((), ())), preferred_element_type=f32
    )


def shift(value, axis, by):
    size = SIZES[axis]
    return lax.ppermute(value, axis, [(i, (i + by) % size) for i in range(size)])


def add(*terms):
    total = terms[0].astype(f32)
    for term in terms[1:]:
        total = total + term.astype(f32)
    return total


def along(blocks, index, axis=0):
    return lax.dynamic_index_in_dim(blocks, index, axis, keepdims=False)


def swap_halves(first, second, index, axis):
    mine = jnp.where(index == 0, first, second)
    other = jnp.where(index == 0, second, first).astype(bf16)
    return add(mine, shift(other, axis, 1))


def ring_send(parts, ring):
    return [shift(parts[k].astype(bf16), ring, k) for k in (2, 1, 3)]


def chip_sum(value, core, axis):
    other = along(value, 1 - core, axis)
    return add(along(value, core, axis), shift(other, "c", 1)).astype(bf16)


def ring_gather(block):
    return [shift(block, "x", -k) for k in (1, 2, 3)]


def shards(
    tokens, cotangent, w_in, w_out, first_moment, rotated_second_moment, left_basis, right_basis
):
    yl, z, c, x, yh = (lax.axis_index(name) for name in ROW + COL)
    both = lax.all_gather(jnp.stack([tokens, cotangent]), ROW, axis=1, tiled=True)
    token_count, width = both.shape[1:]
    rows = token_count // 8
    grad_scale = token_count ** (-0.5)
    gathered = both.reshape(2, 2, 4, rows, width)

    def token_rows(block_x):
        block = lax.dynamic_slice(gathered, (0, 0, block_x, 0, 0), (1, 2, 1, rows, width))
        return block.reshape(2 * rows, width)

    def cot_rows(block_yh, block_x):
        block = lax.dynamic_slice(gathered, (1, block_yh, block_x, 0, 0), (1, 1, 1, rows, width))
        return block.reshape(rows, width)

    def turned(which, block_yh):
        line = lax.dynamic_slice(gathered, (which, block_yh, 0, 0, 0), (1, 1, 4, rows, width))
        line = line.reshape(4 * rows, width)
        return lax.dynamic_slice_in_dim(jnp.concatenate([line, line]), x * rows, 4 * rows, 0)

    def cores_sum(value):
        return chip_sum(value.reshape(4, 2, rows // 2, width), c, 1)

    def by_z(cores):
        return [along(cores, (z - x + j) % 4) for j in range(4)]

    def back_terms(block_yh, offsets):
        block = jnp.concatenate([cot_rows(block_yh, (x + k) % 4) for k in offsets])
        return dot(block, w_out, 1, 1)

    leaving = back_terms(1 - yh, (2, 1, 3)).astype(bf16)
    parts = [None] * 4
    for k in (2, 1, 3):
        parts[k] = dot(token_rows((x + k) % 4), w_in, 1, 0).astype(bf16)
    back_near = shift(leaving, "yh", 1)
    forward_ring = ring_send(parts, "x")
    back_last = shift(back_terms(1 - yh, (0,)).astype(bf16), "yh", 1)
    staying = back_terms(yh, (2, 1, 3))
    staying_last = back_terms(yh, (0,))
    kept = dot(token_rows(x), w_in, 1, 0)
    token_own, token_other = turned(0, yh), turned(0, 1 - yh)
    cot_own, cot_other = turned(1, yh), turned(1, 1 - yh)
    back_near, staying, staying_last, kept, token_own, token_other, cot_own, cot_other = lax.optimization_barrier(
        (back_near, staying, staying_last, kept, token_own, token_other, cot_own, cot_other)
    )

    sums = add(staying, back_near).astype(bf16).reshape(3, rows, width)
    back_ring = ring_send([None, sums[1], sums[0], sums[2]], "x")
    forward_ring, kept, sums = lax.optimization_barrier((forward_ring, kept, sums))

    total = add(kept, *forward_ring).reshape(2, rows, width)
    forward = swap_halves(total[0], total[1], yh, "yh")
    activation, derivative = gelu_pair(forward)
    act = activation.astype(bf16)
    grad = (add(staying_last, back_last, *back_ring) * derivative).astype(bf16)

    act_ring = ring_gather(act)
    act_first = shift(act, "yh", 1)
    pair = shift(grad, "yh", 1)
    grad_ring = ring_gather(grad)
    act_ring, act_first, pair = lax.optimization_barrier((act_ring, act_first, pair))

    act_rest = shift(jnp.concatenate(act_ring), "yh", 1)
    pair_ring = ring_gather(pair)
    grad_ring, act_ring = lax.optimization_barrier((grad_ring, act_ring))

    act_own = jnp.concatenate([act] + act_ring)
    mixed_own = cores_sum(dot(act_own, w_out, 1, 0).astype(bf16))
    grad_own = jnp.concatenate([grad] + grad_ring)
    carried_own = cores_sum(dot(grad_own, w_in, 1, 1).astype(bf16))
    out_grad = dot(act_own, cot_own, 0, 0)
    weight_grad = dot(token_own, grad_own, 0, 0)
    mixed_parts = by_z(mixed_own)
    mixed_arrived = ring_send(mixed_parts, "z")
    act_rest, pair_ring, carried_own, weight_grad, out_grad = lax.optimization_barrier(
        (act_rest, pair_ring, carried_own, weight_grad, out_grad)
    )

    carried_parts = by_z(carried_own)
    carried_arrived = ring_send(carried_parts, "z")
    grad_other = jnp.concatenate([pair] + pair_ring)
    act_other = jnp.concatenate([act_first, act_rest])
    carried_other = cores_sum(dot(grad_other, w_in, 1, 1).astype(bf16))
    mixed_other = cores_sum(dot(act_other, w_out, 1, 0).astype(bf16))
    weight_grad = grad_scale * (weight_grad + dot(token_other, grad_other, 0, 0))
    carried_other, mixed_other, weight_grad = lax.optimization_barrier((carried_other, mixed_other, weight_grad))

    other_parts = [jnp.stack(both) for both in zip(by_z(mixed_other), by_z(carried_other))]
    other_arrived = ring_send(other_parts, "z")
    rounded_grad = weight_grad.astype(bf16)
    left = (dot(rounded_grad, rounded_grad, 1, 1) / HID).astype(bf16)
    left = chip_sum(left.reshape(2, 4, 2, left.shape[0] // 16, left.shape[1]), c, 2)
    right = (dot(rounded_grad, rounded_grad, 0, 0) / D).astype(bf16)
    blocks = right.reshape(4, 2, right.shape[0] // 8, right.shape[1])
    right_parts = [along(blocks, (x + k) % 4) for k in range(4)]
    right_arrived = ring_send(right_parts, "x")
    left, right_parts, carried_arrived, mixed_arrived = lax.optimization_barrier(
        (left, right_parts, carried_arrived, mixed_arrived)
    )

    left_parts = [along(left, (z + j) % 4, 1) for j in range(4)]
    left_arrived = ring_send(left_parts, "z")

    def fine_dot(a, b, ca, cb):
        return lax.dot_general(
            a, b, (((ca,), (cb,)), ((), ())), precision=lax.Precision.HIGH, preferred_element_type=f32
        )

    rotated = fine_dot(fine_dot(left_basis, weight_grad, 0, 0), right_basis, 1, 0)
    new_first = 0.9 * first_moment + 0.1 * rotated
    new_second = 0.95 * rotated_second_moment + 0.05 * rotated * rotated
    ratio = new_first / (jnp.sqrt(new_second) + 1e-08)
    other_arrived, new_first, new_second, ratio = lax.optimization_barrier(
        (other_arrived, new_first, new_second, ratio)
    )

    mine = jnp.stack([add(mixed_parts[0], *mixed_arrived), add(carried_parts[0], *carried_arrived)])
    theirs = add(other_parts[0], *other_arrived)
    tokens_sum = swap_halves(mine, theirs, yl ^ yh, "yl").astype(bf16)
    layer_out, input_grad = tokens_sum[0], tokens_sum[1]
    left = add(left_parts[0], *left_arrived)
    left_stat = swap_halves(left[0], left[1], yl, "yl")
    right = add(right_parts[0], *right_arrived)
    right_stat = swap_halves(right[0], right[1], yh, "yh")
    out_grad = (grad_scale * (out_grad + dot(act_other, cot_other, 0, 0))).astype(bf16)
    update = dot(dot(left_basis, ratio, 1, 0), right_basis, 1, 1)
    return (layer_out, input_grad, out_grad, update, new_first, new_second, left_stat, right_stat)


def solution(mesh):
    fine = Mesh(mesh.devices.reshape(2, 4, 2, 4, 2), ROW + COL)
    in_specs = (
        P(ROW, COL),
        P(ROW, COL),
        P(COL, ROW),
        P(ROW, COL),
        P(COL, ROW),
        P(COL, ROW),
        P(COL, None),
        P(ROW, None),
    )
    out_specs = (
        P(ROW, COL),
        P(ROW, COL),
        P(ROW, COL),
        P(COL, ROW),
        P(COL, ROW),
        P(COL, ROW),
        P(COL + ROW, None),
        P(ROW + COL, None),
    )
    return jax.shard_map(shards, mesh=fine, in_specs=in_specs, out_specs=out_specs, check_vma=False)
```

```python
import jax
import jax.numpy as jnp
from jax import lax
from jax.experimental import pallas as pl
from jax.experimental.pallas import tpu as pltpu
from jax.sharding import Mesh, PartitionSpec as P

D = 6144
HID = 12288

bf16 = jnp.bfloat16
f32 = jnp.float32

ROW = ("yl", "z", "c")
COL = ("x", "yh")
SIZES = {"yl": 2, "z": 4, "c": 2, "x": 4, "yh": 2}


def gelu_pair(hidden):
    normal_cdf = 0.5 * (1.0 + jax.scipy.special.erf(hidden * 0.7071067811865476))
    activation = hidden * normal_cdf
    derivative = normal_cdf + hidden * jnp.exp(-0.5 * hidden * hidden) * 0.3989422804014327
    return (activation, derivative)


def shift(value, axis, by):
    size = SIZES[axis]
    return lax.ppermute(value, axis, [(i, (i + by) % size) for i in range(size)])


def add(*terms):
    total = terms[0].astype(f32)
    for term in terms[1:]:
        total = total + term.astype(f32)
    return total


def matmul(a, b, ca=1, cb=0):
    return lax.dot_general(a, b, (((ca,), (cb,)), ((), ())), preferred_element_type=f32)


def ring_send(parts, ring):
    return [shift(parts[k].astype(bf16), ring, k) for k in (2, 1, 3)]


def ring_gather(block):
    return [shift(block, "x", -k) for k in (1, 2, 3)]


def whole(shape):
    return pl.BlockSpec(shape, lambda *_: (0,) * len(shape))


def call(kernel, scalars, grid, in_specs, out_specs, out_shape, scratch, flops, *args):
    moved = sum(v.size * v.dtype.itemsize for v in args) + sum(
        v.size * jnp.dtype(v.dtype).itemsize for v in jax.tree.leaves(out_shape)
    )
    return pl.pallas_call(
        kernel,
        out_shape=out_shape,
        grid_spec=pltpu.PrefetchScalarGridSpec(
            num_scalar_prefetch=1,
            grid=grid,
            in_specs=in_specs,
            out_specs=out_specs,
            scratch_shapes=scratch,
        ),
        compiler_params=pltpu.CompilerParams(vmem_limit_bytes=50 * 2**20),
        cost_estimate=pl.CostEstimate(flops=flops, bytes_accessed=moved, transcendentals=0),
    )(jnp.stack([jnp.asarray(v, jnp.int32) for v in scalars]), *args)


def pair_dot(source, blocks, weight, cb, dtype, joined):
    rows, width = source.shape[1:]
    pairs = len(blocks) // 2
    out = jax.ShapeDtypeStruct((2 * pairs if joined else 2, rows, weight.shape[1 - cb]), dtype)

    def kernel(_, first, second, w_ref, *outs):
        both = jnp.concatenate([first[0], second[0]])
        result = matmul(both, w_ref[...], 1, cb).astype(dtype).reshape((2,) + out.shape[1:])
        if joined:
            outs[0][...] = result
            return
        for i in range(pairs):

            @pl.when(pl.program_id(0) == i)
            def _():
                outs[i][...] = result

    block = (2,) + out.shape[1:]
    return call(
        kernel,
        blocks,
        (pairs,),
        [
            pl.BlockSpec((1, rows, width), lambda i, at: (at[2 * i], 0, 0)),
            pl.BlockSpec((1, rows, width), lambda i, at: (at[2 * i + 1], 0, 0)),
            whole(weight.shape),
        ],
        [pl.BlockSpec(block, lambda i, at: (i, 0, 0))] if joined else [whole(block)] * pairs,
        [out] * (1 if joined else pairs),
        [],
        4 * pairs * rows * weight.size,
        source,
        source,
        weight,
    )


def token_terms(acts, grads, w_out, w_in, turn, first, split):
    rows, width = acts[0].shape
    half = rows // 2
    acts, grads = ([v.reshape(2, half, width) for v in group] for group in (acts, grads))

    def kernel(at, *refs):
        w_out_ref, w_in_ref = refs[8:10]
        outs = refs[10:]
        core = at[1]
        for k in range(4):

            @pl.when(pl.program_id(0) == k)
            def _():
                for kind, (ref, w_ref, cb) in enumerate(((refs[k], w_out_ref, 0), (refs[4 + k], w_in_ref, 1))):
                    both = jnp.concatenate([ref[core], ref[1 - core]])
                    result = matmul(both, w_ref[...], 1, cb).astype(bf16)
                    for i in range(2):
                        piece = result[i * half : (i + 1) * half]
                        if split:
                            outs[i][0, kind] = piece
                        else:
                            outs[0][0, i, kind] = piece

    place = lambda k, at: (lax.rem(at[0] + k, 4),)
    block = (2, half, width) if split else (2, 2, half, width)
    spec = pl.BlockSpec((1,) + block, lambda k, at: place(k, at) + (0,) * len(block))
    out = jax.ShapeDtypeStruct((4,) + block, bf16)
    count = 2 if split else 1
    return call(
        kernel,
        [turn, first],
        (4,),
        [whole((2, half, width))] * 8 + [whole(w_out.shape), whole(w_in.shape)],
        [spec] * count,
        [out] * count,
        [],
        16 * rows * width * width,
        *acts,
        *grads,
        w_out,
        w_in,
    )


def gram_terms(partial, token_other, grads, scale, z, c, x, yh):
    size = partial.shape[0]
    left_rows, right_rows = size // 16, size // 8

    def kernel(at, part_ref, token_ref, *refs):
        grad_refs, refs = refs[:4], refs[4:]
        weight_ref, send_ref, keep_ref = refs[:3]
        right_refs, (rounded, left, right) = refs[3:7], refs[7:]
        grad = jnp.concatenate([ref[...] for ref in grad_refs])
        weight = scale * (part_ref[...] + matmul(token_ref[...], grad, 0, 0))
        weight_ref[...] = weight
        rounded[...] = weight.astype(bf16)
        here = rounded[...]
        left[...] = (matmul(here, here, 1, 1) * (1.0 / HID)).reshape(16, left_rows, size)
        right[...] = (matmul(here, here, 0, 0) * (1.0 / D)).reshape(8, right_rows, size)
        for k in range(4):
            along_z, along_x = lax.rem(at[0] + k, 4), lax.rem(at[2] + k, 4)
            for y in range(2):
                row = y * 8 + along_z * 2
                send_ref[k, y] = left[row + 1 - at[1]].astype(bf16)
                keep_ref[k, y] = left[row + at[1]].astype(bf16)
                other = at[3] if y == 0 else 1 - at[3]
                right_refs[k][y] = right[along_x * 2 + other].astype(bf16)

    shapes = [(size, size)] + [(4, 2, left_rows, size)] * 2 + [(2, right_rows, size)] * 4
    return call(
        kernel,
        [z, c, x, yh],
        (1,),
        [whole(v.shape) for v in (partial, token_other, *grads)],
        [whole(v) for v in shapes],
        [jax.ShapeDtypeStruct(v, f32 if i == 0 else bf16) for i, v in enumerate(shapes)],
        [
            pltpu.VMEM((size, size), bf16),
            pltpu.VMEM((16, left_rows, size), f32),
            pltpu.VMEM((8, right_rows, size), f32),
        ],
        4 * size**3 + 2 * token_other.size * size,
        partial,
        token_other,
        *grads,
    )


def core_sums(*pairs):
    width = pairs[0].shape[-1]
    pairs = [v.reshape(4, -1, width) for v in pairs]
    counts = [v.shape[1] for v in pairs[::2]]

    def kernel(_, *refs):
        ins, outs = refs[: len(pairs)], refs[len(pairs) :]
        for k in range(4):
            start = 0
            for i, count in enumerate(counts):
                total = ins[2 * i][k].astype(f32) + ins[2 * i + 1][k].astype(f32)
                outs[k][start : start + count] = total.astype(outs[k].dtype)
                start += count

    shape = (sum(counts), width)
    return call(
        kernel,
        [0],
        (1,),
        [whole(v.shape) for v in pairs],
        [whole(shape)] * 4,
        [jax.ShapeDtypeStruct(shape, bf16 if k else f32) for k in range(4)],
        [],
        0,
        *pairs,
    )


def rotated_step(weight_grad, left_basis, right_basis, first_moment, second_moment):
    size = weight_grad.shape[0]
    parts = 3 if size % 384 == 0 else 1
    cut = size // parts

    def two(value):
        high = value.astype(bf16)
        return high, (value - high.astype(f32)).astype(bf16)

    def fine(a, b, ca, cb):
        return matmul(a[0], b[0], ca, cb) + (matmul(a[0], b[1], ca, cb) + matmul(a[1], b[0], ca, cb))

    def kernel(_, w_ref, l_ref, r_ref, m_ref, v_ref, first_ref, second_ref, update_ref, turned):
        step = pl.program_id(0)

        @pl.when(step == 0)
        def _():
            turned[...] = fine(two(l_ref[...]), two(w_ref[...]), 0, 0)

        right = two(r_ref[...])
        rotated = fine(two(turned[...]), right, 1, 0)
        new_first = 0.9 * m_ref[...] + 0.1 * rotated
        new_second = 0.95 * v_ref[...] + 0.05 * rotated * rotated
        first_ref[...] = new_first
        second_ref[...] = new_second
        ratio = new_first / (jnp.sqrt(new_second) + 1e-08)
        back = matmul(l_ref[...].astype(bf16), ratio.astype(bf16))
        update = matmul(back.astype(bf16), right[0], 1, 1)

        @pl.when(step == 0)
        def _():
            update_ref[...] = update

        @pl.when(step > 0)
        def _():
            update_ref[...] += update

    columns = pl.BlockSpec((size, cut), lambda i, _: (0, i))
    out = jax.ShapeDtypeStruct((size, size), f32)
    return call(
        kernel,
        [0],
        (parts,),
        [whole((size, size))] * 2 + [columns] * 3,
        [columns, columns, whole((size, size))],
        [out] * 3,
        [pltpu.VMEM((size, size), f32)],
        16 * size**3,
        weight_grad,
        left_basis,
        right_basis,
        first_moment,
        second_moment,
    )


def shards(
    tokens, cotangent, w_in, w_out, first_moment, rotated_second_moment, left_basis, right_basis
):
    yl, z, c, x, yh = (lax.axis_index(name) for name in ROW + COL)
    both = lax.all_gather(jnp.stack([tokens, cotangent]), ROW, axis=1, tiled=True)
    token_count, width = both.shape[1:]
    rows = token_count // 8
    grad_scale = token_count ** (-0.5)
    gathered = both.reshape(16, rows, width)

    def at(kind, block_yh, k):
        return kind * 8 + block_yh * 4 + (x + k) % 4

    def turned(kind, block_yh):
        line = lax.dynamic_slice_in_dim(gathered, kind * 8 + block_yh * 4, 4, 0).reshape(4 * rows, width)
        return lax.dynamic_slice_in_dim(jnp.concatenate([line, line]), x * rows, 4 * rows, 0)

    (leaving,) = pair_dot(gathered, [at(1, 1 - yh, k) for k in range(4)], w_out, 1, bf16, True)
    back_arrived = shift(leaving, "yh", 1)
    leaving, w_in_later = lax.optimization_barrier((leaving, w_in))
    places = [at(0, place, k) for k in (2, 1, 3) for place in (yh, 1 - yh)]
    two, one, three = pair_dot(gathered, places, w_in_later, 0, bf16, False)
    arrived = ring_send([None, one, two, three], "x")
    (staying,) = pair_dot(gathered, [at(1, yh, k) for k in range(4)], w_out, 1, f32, True)
    (kept,) = pair_dot(gathered, [at(0, yh, 0), at(0, 1 - yh, 0)], w_in_later, 0, f32, True)
    token_own, token_other = turned(0, yh), turned(0, 1 - yh)
    cot_own, cot_other = turned(1, yh), turned(1, 1 - yh)
    arrived, back_arrived, kept, staying, token_own, token_other, cot_own, cot_other = lax.optimization_barrier(
        (arrived, back_arrived, kept, staying, token_own, token_other, cot_own, cot_other)
    )

    other = add(kept[1], *[v[1] for v in arrived]).astype(bf16)
    other = shift(other, "yh", 1)
    back = ring_send([add(staying[k], back_arrived[k]) for k in range(4)], "x")
    forward = add(kept[0], *[v[0] for v in arrived], other)
    activation, derivative = gelu_pair(forward)
    act = activation.astype(bf16)
    back, act, derivative = lax.optimization_barrier((back, act, derivative))

    acts = ring_gather(act)
    grad = (add(staying[0], back_arrived[0], *back) * derivative).astype(bf16)
    pair = shift(grad, "yh", 1)
    act_pair = shift(act, "yh", 1)
    acts, grad, pair, act_pair = lax.optimization_barrier((acts, grad, pair, act_pair))

    grads = ring_gather(grad)
    act_pairs = [act_pair, shift(acts[0], "yh", 1), shift(acts[1], "yh", 1)]
    grads, act_pairs, acts, pair = lax.optimization_barrier((grads, act_pairs, acts, pair))

    pairs = [pair] + ring_gather(pair)
    act_pairs.append(shift(acts[2], "yh", 1))
    acts, grads = [act] + acts, [grad] + grads
    (own,) = token_terms(acts, grads, w_out, w_in, x, 0, False)
    own = lax.psum_scatter(own.reshape(token_count, width), ("z", "c"), scatter_dimension=0, tiled=True)
    out_grad = matmul(jnp.concatenate(acts), cot_own, 0, 0)
    weight_grad = matmul(token_own, jnp.concatenate(grads), 0, 0)
    pairs, act_pairs, weight_grad, out_grad = lax.optimization_barrier((pairs, act_pairs, weight_grad, out_grad))

    send, keep = token_terms(act_pairs, pairs, w_out, w_in, x + 4 - z, 1 - c, True)
    core_arrived = shift(send, "c", 1)
    send, token_later = lax.optimization_barrier((send, token_other))
    weight_grad, left_send, left_keep, *right = gram_terms(
        weight_grad, token_later, pairs, grad_scale, z, c, x, yh
    )
    left_arrived = shift(left_send, "c", 1)
    core_arrived, left_arrived, right, weight_grad = lax.optimization_barrier(
        (core_arrived, left_arrived, right, weight_grad)
    )

    chip = core_sums(keep, core_arrived, left_keep, left_arrived)
    chip_arrived = ring_send(chip, "z")
    right_arrived = ring_send(right, "x")
    chip, weight_grad = lax.optimization_barrier((chip, weight_grad))
    new_first, new_second, update = rotated_step(
        weight_grad, left_basis, right_basis, first_moment, rotated_second_moment
    )
    chip_arrived, update, own = lax.optimization_barrier((chip_arrived, update, own))

    total = add(chip[0], *chip_arrived)
    theirs, left = total[:rows], total[rows:]
    own = own.astype(f32)
    left_rows = left.shape[0] // 2
    same = yl == yh
    keep = jnp.concatenate(
        [jnp.where(same, own, theirs), jnp.where(yl == 0, left[:left_rows], left[left_rows:])]
    )
    send = jnp.concatenate(
        [jnp.where(same, theirs, own), jnp.where(yl == 0, left[left_rows:], left[:left_rows])]
    )
    last = add(keep, shift(send.astype(bf16), "yl", 1))
    layer_out = last[: rows // 2].astype(bf16)
    input_grad = last[rows // 2 : rows].astype(bf16)
    left_stat = last[rows:]
    right_own = add(*[v[0] for v in (right[0], *right_arrived)])
    right_other = add(*[v[1] for v in (right[0], *right_arrived)]).astype(bf16)
    right_stat = add(right_own, shift(right_other, "yh", 1))
    out_grad = (grad_scale * (out_grad + matmul(jnp.concatenate(act_pairs), cot_other, 0, 0))).astype(bf16)
    return (layer_out, input_grad, out_grad, update, new_first, new_second, left_stat, right_stat)


def solution(mesh):
    fine = Mesh(mesh.devices.reshape(2, 4, 2, 4, 2), ROW + COL)
    in_specs = (
        P(ROW, COL),
        P(ROW, COL),
        P(COL, ROW),
        P(ROW, COL),
        P(COL, ROW),
        P(COL, ROW),
        P(COL, None),
        P(ROW, None),
    )
    out_specs = (
        P(ROW, COL),
        P(ROW, COL),
        P(ROW, COL),
        P(COL, ROW),
        P(COL, ROW),
        P(COL, ROW),
        P(COL + ROW, None),
        P(ROW + COL, None),
    )
    return jax.shard_map(shards, mesh=fine, in_specs=in_specs, out_specs=out_specs, check_vma=False)
```

```python
import jax
import jax.numpy as jnp
from jax import lax
from jax.experimental import pallas as pl
from jax.experimental.pallas import tpu as pltpu
from jax.sharding import Mesh, PartitionSpec as P

D = 6144
HID = 12288

bf16 = jnp.bfloat16
f32 = jnp.float32

ROW = ("yl", "z", "c")
COL = ("x", "yh")
SIZES = {"yl": 2, "z": 4, "c": 2, "x": 4, "yh": 2}


def gelu_pair(hidden):
    normal_cdf = 0.5 * (1.0 + jax.scipy.special.erf(hidden * 0.7071067811865476))
    activation = hidden * normal_cdf
    derivative = normal_cdf + hidden * jnp.exp(-0.5 * hidden * hidden) * 0.3989422804014327
    return (activation, derivative)


def shift(value, axis, by):
    size = SIZES[axis]
    return lax.ppermute(value, axis, [(i, (i + by) % size) for i in range(size)])


def add(*terms):
    total = terms[0].astype(f32)
    for term in terms[1:]:
        total = total + term.astype(f32)
    return total


def matmul(a, b, ca=1, cb=0):
    return lax.dot_general(a, b, (((ca,), (cb,)), ((), ())), preferred_element_type=f32)


def ring_send(parts, ring):
    return [shift(parts[k].astype(bf16), ring, k) for k in (2, 1, 3)]


def ring_gather(block):
    return [shift(block, "x", -k) for k in (1, 2, 3)]


def whole(shape):
    return pl.BlockSpec(shape, lambda *_: (0,) * len(shape))


def call(kernel, scalars, grid, in_specs, out_specs, out_shape, scratch, flops, *args):
    moved = sum(v.size * v.dtype.itemsize for v in args) + sum(
        v.size * jnp.dtype(v.dtype).itemsize for v in jax.tree.leaves(out_shape)
    )
    return pl.pallas_call(
        kernel,
        out_shape=out_shape,
        grid_spec=pltpu.PrefetchScalarGridSpec(
            num_scalar_prefetch=1,
            grid=grid,
            in_specs=in_specs,
            out_specs=out_specs,
            scratch_shapes=scratch,
        ),
        compiler_params=pltpu.CompilerParams(vmem_limit_bytes=50 * 2**20),
        cost_estimate=pl.CostEstimate(flops=flops, bytes_accessed=moved, transcendentals=0),
    )(jnp.stack([jnp.asarray(v, jnp.int32) for v in scalars]), *args)


def pair_dot(source, blocks, weight, cb, dtype, joined):
    rows, width = source.shape[1:]
    pairs = len(blocks) // 2
    out = jax.ShapeDtypeStruct((2 * pairs if joined else 2, rows, weight.shape[1 - cb]), dtype)

    def kernel(_, first, second, w_ref, *outs):
        both = jnp.concatenate([first[0], second[0]])
        result = matmul(both, w_ref[...], 1, cb).astype(dtype).reshape((2,) + out.shape[1:])
        if joined:
            outs[0][...] = result
            return
        for i in range(pairs):

            @pl.when(pl.program_id(0) == i)
            def _():
                outs[i][...] = result

    block = (2,) + out.shape[1:]
    return call(
        kernel,
        blocks,
        (pairs,),
        [
            pl.BlockSpec((1, rows, width), lambda i, at: (at[2 * i], 0, 0)),
            pl.BlockSpec((1, rows, width), lambda i, at: (at[2 * i + 1], 0, 0)),
            whole(weight.shape),
        ],
        [pl.BlockSpec(block, lambda i, at: (i, 0, 0))] if joined else [whole(block)] * pairs,
        [out] * (1 if joined else pairs),
        [],
        4 * pairs * rows * weight.size,
        source,
        source,
        weight,
    )


def token_terms(kinds, turn, first, split):
    rows, width = kinds[0][0][0][0].shape[1:]
    half, number = rows // 2, len(kinds)
    places = [place for group, _ in kinds for _, place in group]
    blocks = [v.reshape(-1, 2, half, width) for group, _ in kinds for v, _ in group]
    weights = [weight for _, weight in kinds]

    def kernel(at, *refs):
        weight_refs, outs = refs[4 * number : 5 * number], refs[5 * number :]
        core = at[1]
        for k in range(4):

            @pl.when(pl.program_id(0) == k)
            def _():
                for kind in range(number):
                    ref = refs[4 * kind + k]
                    both = jnp.concatenate([ref[0, core], ref[0, 1 - core]])
                    result = matmul(both, weight_refs[kind][...]).astype(bf16)
                    for i in range(2):
                        piece = result[i * half : (i + 1) * half]
                        if split:
                            outs[i][0, kind] = piece
                        else:
                            outs[0][0, i, kind] = piece

    block = (number, half, width) if split else (2, number, half, width)
    spec = pl.BlockSpec((1,) + block, lambda k, at: (lax.rem(at[0] + k, 4),) + (0,) * len(block))
    out = jax.ShapeDtypeStruct((4,) + block, bf16)
    count = 2 if split else 1
    return call(
        kernel,
        [turn, first],
        (4,),
        [pl.BlockSpec((1, 2, half, width), lambda k, _, place=place: (place, 0, 0, 0)) for place in places]
        + [whole(v.shape) for v in weights],
        [spec] * count,
        [out] * count,
        [],
        8 * number * rows * width * width,
        *blocks,
        *weights,
    )


def accumulate(lines, pieces):
    size = lines.shape[1]

    def kernel(_, *refs):
        lines_ref, out_ref = refs[0], refs[-1]
        total = matmul(lines_ref[pieces[0][0]], refs[1][...])
        for i, (k, _) in enumerate(pieces[1:]):
            total = total + matmul(lines_ref[k], refs[2 + i][...])
        out_ref[...] = total

    out = (size, pieces[0][1].shape[1])
    return call(
        kernel,
        [0],
        (1,),
        [whole(lines.shape)] + [whole(v.shape) for _, v in pieces],
        whole(out),
        jax.ShapeDtypeStruct(out, f32),
        [],
        2 * len(pieces) * size * pieces[0][1].size,
        lines,
        *[v for _, v in pieces],
    )


def gram_terms(partial, line, piece, scale, z, c, x, yh):
    size = partial.shape[0]
    left_rows, right_rows = size // 16, size // 8

    def kernel(at, part_ref, line_ref, piece_ref, *refs):
        weight_ref, send_ref, keep_ref = refs[:3]
        right_refs, (left, right) = refs[3:7], refs[7:]
        weight = scale * (part_ref[...] + matmul(line_ref[...], piece_ref[...]))
        weight_ref[...] = weight
        here, turned = weight.astype(bf16), weight.T.astype(bf16)
        left[...] = (matmul(here, turned) * (1.0 / HID)).reshape(16, left_rows, size)
        right[...] = (matmul(turned, here) * (1.0 / D)).reshape(8, right_rows, size)
        for k in range(4):
            along_z, along_x = lax.rem(at[0] + k, 4), lax.rem(at[2] + k, 4)
            for y in range(2):
                row = y * 8 + along_z * 2
                send_ref[k, y] = left[row + 1 - at[1]].astype(bf16)
                keep_ref[k, y] = left[row + at[1]].astype(bf16)
                other = at[3] if y == 0 else 1 - at[3]
                right_refs[k][y] = right[along_x * 2 + other].astype(bf16)

    shapes = [(size, size)] + [(4, 2, left_rows, size)] * 2 + [(2, right_rows, size)] * 4
    return call(
        kernel,
        [z, c, x, yh],
        (1,),
        [whole(v.shape) for v in (partial, line, piece)],
        [whole(v) for v in shapes],
        [jax.ShapeDtypeStruct(v, f32 if i == 0 else bf16) for i, v in enumerate(shapes)],
        [
            pltpu.VMEM((16, left_rows, size), f32),
            pltpu.VMEM((8, right_rows, size), f32),
        ],
        4 * size**3 + 2 * line.size * size,
        partial,
        line,
        piece,
    )


def core_sums(*pairs):
    width = pairs[0].shape[-1]
    pairs = [v.reshape(4, -1, width) for v in pairs]
    counts = [v.shape[1] for v in pairs[::2]]

    def kernel(_, *refs):
        ins, outs = refs[: len(pairs)], refs[len(pairs) :]
        for k in range(4):
            start = 0
            for i, count in enumerate(counts):
                total = ins[2 * i][k].astype(f32) + ins[2 * i + 1][k].astype(f32)
                outs[k][start : start + count] = total.astype(outs[k].dtype)
                start += count

    shape = (sum(counts), width)
    return call(
        kernel,
        [0],
        (1,),
        [whole(v.shape) for v in pairs],
        [whole(shape)] * 4,
        [jax.ShapeDtypeStruct(shape, bf16 if k else f32) for k in range(4)],
        [],
        0,
        *pairs,
    )


def rotated_step(weight_grad, left_basis, left_turned, right_basis, first_moment, second_moment):
    size = weight_grad.shape[0]
    parts = 3 if size % 384 == 0 else 1
    cut = size // parts

    def two(value):
        high = value.astype(bf16)
        return high, (value - high.astype(f32)).astype(bf16)

    def fine(a, b, ca, cb):
        return matmul(a[0], b[0], ca, cb) + (matmul(a[0], b[1], ca, cb) + matmul(a[1], b[0], ca, cb))

    def kernel(_, w_ref, l_ref, t_ref, r_ref, m_ref, v_ref, first_ref, second_ref, update_ref, turned):
        step = pl.program_id(0)

        @pl.when(step == 0)
        def _():
            turned[...] = fine(two(t_ref[...]), two(w_ref[...]), 1, 0)

        right = two(r_ref[...])
        rotated = fine(two(turned[...]), right, 1, 0)
        new_first = 0.9 * m_ref[...] + 0.1 * rotated
        new_second = 0.95 * v_ref[...] + 0.05 * rotated * rotated
        first_ref[...] = new_first
        second_ref[...] = new_second
        ratio = new_first / (jnp.sqrt(new_second) + 1e-08)
        back = matmul(l_ref[...].astype(bf16), ratio.astype(bf16))
        update = matmul(back.astype(bf16), right[0], 1, 1)

        @pl.when(step == 0)
        def _():
            update_ref[...] = update

        @pl.when(step > 0)
        def _():
            update_ref[...] += update

    columns = pl.BlockSpec((size, cut), lambda i, _: (0, i))
    out = jax.ShapeDtypeStruct((size, size), f32)
    return call(
        kernel,
        [0],
        (parts,),
        [whole((size, size))] * 3 + [columns] * 3,
        [columns, columns, whole((size, size))],
        [out] * 3,
        [pltpu.VMEM((size, size), f32)],
        16 * size**3,
        weight_grad,
        left_basis,
        left_turned,
        right_basis,
        first_moment,
        second_moment,
    )


def shards(
    tokens, cotangent, w_in, w_out, first_moment, rotated_second_moment, left_basis, right_basis
):
    yl, z, c, x, yh = (lax.axis_index(name) for name in ROW + COL)
    both = lax.all_gather(jnp.stack([tokens, cotangent]), ROW, axis=1, tiled=True)
    token_count, width = both.shape[1:]
    rows = token_count // 8
    grad_scale = token_count ** (-0.5)
    gathered = both.reshape(16, rows, width)

    def at(kind, block_yh, k):
        return kind * 8 + block_yh * 4 + (x + k) % 4

    def turned(kind):
        return jnp.concatenate(
            [lax.dynamic_index_in_dim(gathered, at(kind, y, k), 0, False) for k in range(4) for y in (yh, 1 - yh)]
        )

    w_in_turned, w_out_turned, left_turned = lax.optimization_barrier((w_in.T, w_out.T, left_basis.T))

    (leaving,) = pair_dot(gathered, [at(1, 1 - yh, k) for k in range(4)], w_out_turned, 0, bf16, True)
    back_arrived = shift(leaving, "yh", 1)
    leaving, w_in_later = lax.optimization_barrier((leaving, w_in))
    (two,) = pair_dot(gathered, [at(0, yh, 2), at(0, 1 - yh, 2)], w_in_later, 0, bf16, True)
    places = [at(0, place, k) for k in (1, 3) for place in (yh, 1 - yh)]
    two_sent, w_in_later = lax.optimization_barrier((two, w_in_later))
    one, three = pair_dot(gathered, places, w_in_later, 0, bf16, False)
    arrived = ring_send([None, one, two_sent, three], "x")
    (staying,) = pair_dot(gathered, [at(1, yh, k) for k in range(4)], w_out_turned, 0, f32, True)
    (kept,) = pair_dot(gathered, [at(0, yh, 0), at(0, 1 - yh, 0)], w_in_later, 0, f32, True)
    token_turned = turned(0).reshape(4, 2 * rows, width).swapaxes(1, 2)
    cots = turned(1).reshape(4, 2, rows, width).swapaxes(0, 1).reshape(2, 4 * rows, width)
    arrived, back_arrived, kept, staying, token_turned, cots = lax.optimization_barrier(
        (arrived, back_arrived, kept, staying, token_turned, cots)
    )

    other = add(kept[1], *[v[1] for v in arrived]).astype(bf16)
    other = shift(other, "yh", 1)
    back = ring_send([add(staying[k], back_arrived[k]) for k in range(4)], "x")
    forward = add(kept[0], *[v[0] for v in arrived], other)
    activation, derivative = gelu_pair(forward)
    act = activation.astype(bf16)
    back, act, derivative = lax.optimization_barrier((back, act, derivative))

    acts = ring_gather(act)
    grad = (add(staying[0], back_arrived[0], *back) * derivative).astype(bf16)
    pair = shift(grad, "yh", 1)
    acts, grad, pair = lax.optimization_barrier((acts, grad, pair))

    act_own = jnp.concatenate([act] + acts)
    act_other = shift(act_own, "yh", 1)
    grad_both = jnp.concatenate([grad, pair])
    one, two, three = ring_gather(grad_both)
    one, act_own, acts, grad_both = lax.optimization_barrier((one, act_own, acts, grad_both))

    def sum_zc(blocks, weight):
        (terms,) = token_terms([(blocks, weight)], x, 0, False)
        return lax.psum_scatter(terms.reshape(-1, width), ("z", "c"), scatter_dimension=0, tiled=True)

    mixed_own = sum_zc([(v[None], 0) for v in [act] + acts], w_out)
    out_grad = matmul(act_own, cots[0], 0, 0)
    one, three, out_grad = lax.optimization_barrier((one, three, out_grad))
    weight_grad = accumulate(token_turned, [(0, grad_both), (1, one), (3, three)])
    two, act_other, weight_grad, out_grad = lax.optimization_barrier((two, act_other, weight_grad, out_grad))

    grads = [v.reshape(2, rows, width) for v in (grad_both, one, two, three)]
    acts = act_other.reshape(4, rows, width)
    kinds = [([(acts, k) for k in range(4)], w_out), ([(v, 1) for v in grads], w_in_turned)]
    send, keep = token_terms(kinds, x + 4 - z, 1 - c, True)
    core_arrived = shift(send, "c", 1)
    send, two = lax.optimization_barrier((send, two))
    weight_grad, left_send, left_keep, *right = gram_terms(
        weight_grad, token_turned[2], two, grad_scale, z, c, x, yh
    )
    left_arrived = shift(left_send, "c", 1)
    left_send, grads = lax.optimization_barrier((left_send, grads))
    carried_own = sum_zc([(v, 0) for v in grads], w_in_turned)
    core_arrived, left_arrived, right, weight_grad = lax.optimization_barrier(
        (core_arrived, left_arrived, right, weight_grad)
    )

    chip = core_sums(keep, core_arrived, left_keep, left_arrived)
    chip_arrived = ring_send(chip, "z")
    chip, right, weight_grad, act_other = lax.optimization_barrier((chip, right, weight_grad, act_other))
    right_arrived = ring_send(right, "x")
    new_first, new_second, update = rotated_step(
        weight_grad, left_basis, left_turned, right_basis, first_moment, rotated_second_moment
    )
    out_grad = (grad_scale * (out_grad + matmul(act_other, cots[1], 0, 0))).astype(bf16)
    chip_arrived, update, mixed_own, carried_own = lax.optimization_barrier(
        (chip_arrived, update, mixed_own, carried_own)
    )

    total = add(chip[0], *chip_arrived)
    theirs, left = total[:rows], total[rows:]
    own = jnp.concatenate([mixed_own, carried_own]).astype(f32)
    left_rows = left.shape[0] // 2
    same = yl == yh
    keep = jnp.concatenate(
        [jnp.where(same, own, theirs), jnp.where(yl == 0, left[:left_rows], left[left_rows:])]
    )
    send = jnp.concatenate(
        [jnp.where(same, theirs, own), jnp.where(yl == 0, left[left_rows:], left[:left_rows])]
    )
    last = add(keep, shift(send.astype(bf16), "yl", 1))
    layer_out = last[: rows // 2].astype(bf16)
    input_grad = last[rows // 2 : rows].astype(bf16)
    left_stat = last[rows:]
    right_own = add(*[v[0] for v in (right[0], *right_arrived)])
    right_other = add(*[v[1] for v in (right[0], *right_arrived)]).astype(bf16)
    right_stat = add(right_own, shift(right_other, "yh", 1))
    return (layer_out, input_grad, out_grad, update, new_first, new_second, left_stat, right_stat)


def solution(mesh):
    fine = Mesh(mesh.devices.reshape(2, 4, 2, 4, 2), ROW + COL)
    in_specs = (
        P(ROW, COL),
        P(ROW, COL),
        P(COL, ROW),
        P(ROW, COL),
        P(COL, ROW),
        P(COL, ROW),
        P(COL, None),
        P(ROW, None),
    )
    out_specs = (
        P(ROW, COL),
        P(ROW, COL),
        P(ROW, COL),
        P(COL, ROW),
        P(COL, ROW),
        P(COL, ROW),
        P(COL + ROW, None),
        P(ROW + COL, None),
    )
    return jax.shard_map(shards, mesh=fine, in_specs=in_specs, out_specs=out_specs, check_vma=False)
```

```python
import jax
import jax.numpy as jnp
from jax import lax
from jax.experimental import pallas as pl
from jax.experimental.pallas import tpu as pltpu
from jax.sharding import Mesh, PartitionSpec as P

D = 6144
HID = 12288

bf16 = jnp.bfloat16
f32 = jnp.float32

ROW = ("yl", "z", "c")
COL = ("x", "yh")
SIZES = {"yl": 2, "z": 4, "c": 2, "x": 4, "yh": 2}


def gelu_pair(hidden):
    normal_cdf = 0.5 * (1.0 + jax.scipy.special.erf(hidden * 0.7071067811865476))
    activation = hidden * normal_cdf
    derivative = normal_cdf + hidden * jnp.exp(-0.5 * hidden * hidden) * 0.3989422804014327
    return (activation, derivative)


def shift(value, axis, by):
    size = SIZES[axis]
    return lax.ppermute(value, axis, [(i, (i + by) % size) for i in range(size)])


def add(*terms):
    total = terms[0].astype(f32)
    for term in terms[1:]:
        total = total + term.astype(f32)
    return total


def matmul(a, b, ca=1, cb=0):
    return lax.dot_general(a, b, (((ca,), (cb,)), ((), ())), preferred_element_type=f32)


def ring_send(parts, ring):
    return [shift(parts[k].astype(bf16), ring, k) for k in (2, 1, 3)]


def ring_gather(block):
    return [shift(block, "x", -k) for k in (1, 2, 3)]


def whole(shape):
    return pl.BlockSpec(shape, lambda *_: (0,) * len(shape))


def call(kernel, scalars, grid, in_specs, out_specs, out_shape, scratch, flops, *args):
    moved = sum(v.size * v.dtype.itemsize for v in args) + sum(
        v.size * jnp.dtype(v.dtype).itemsize for v in jax.tree.leaves(out_shape)
    )
    return pl.pallas_call(
        kernel,
        out_shape=out_shape,
        grid_spec=pltpu.PrefetchScalarGridSpec(
            num_scalar_prefetch=1,
            grid=grid,
            in_specs=in_specs,
            out_specs=out_specs,
            scratch_shapes=scratch,
        ),
        compiler_params=pltpu.CompilerParams(vmem_limit_bytes=50 * 2**20),
        cost_estimate=pl.CostEstimate(flops=flops, bytes_accessed=moved, transcendentals=0),
    )(jnp.stack([jnp.asarray(v, jnp.int32) for v in scalars]), *args)


def gram_terms(weight_grad, z, c, x, yh):
    size = weight_grad.shape[0]
    left_rows, right_rows = size // 16, size // 8

    def kernel(at, weight_ref, *refs):
        send_ref, keep_ref = refs[:2]
        right_refs, (left, right) = refs[2:6], refs[6:]
        weight = weight_ref[...]
        here, turned = weight.astype(bf16), weight.T.astype(bf16)
        left[...] = (matmul(here, turned) * (1.0 / HID)).reshape(16, left_rows, size)
        right[...] = (matmul(turned, here) * (1.0 / D)).reshape(8, right_rows, size)
        for k in range(4):
            along_z, along_x = lax.rem(at[0] + k, 4), lax.rem(at[2] + k, 4)
            for y in range(2):
                row = y * 8 + along_z * 2
                send_ref[k, y] = left[row + 1 - at[1]].astype(bf16)
                keep_ref[k, y] = left[row + at[1]].astype(bf16)
                other = at[3] if y == 0 else 1 - at[3]
                right_refs[k][y] = right[along_x * 2 + other].astype(bf16)

    shapes = [(4, 2, left_rows, size)] * 2 + [(2, right_rows, size)] * 4
    return call(
        kernel,
        [z, c, x, yh],
        (1,),
        [whole((size, size))],
        [whole(v) for v in shapes],
        [jax.ShapeDtypeStruct(v, bf16) for v in shapes],
        [
            pltpu.VMEM((16, left_rows, size), f32),
            pltpu.VMEM((8, right_rows, size), f32),
        ],
        4 * size**3,
        weight_grad,
    )


def core_sums(z, c, tokens, left):
    width = left[0].shape[-1]
    left = [v.reshape(4, -1, width) for v in left]
    rows = tokens[0][1].shape[2] if tokens else 0
    shape = (2 * len(tokens) * rows + left[0].shape[1], width)
    args = [v for pair in tokens for v in pair] + left

    def kernel(at, *refs):
        ins, outs = refs[: len(args)], refs[len(args) :]
        for k in range(4):
            place = lax.rem(at[0] + k, 4)
            start = 0
            for i in range(len(tokens)):
                for y in range(2):
                    total = ins[2 * i][y, place, at[1]].astype(f32) + ins[2 * i + 1][y, place].astype(f32)
                    outs[k][start : start + rows] = total.astype(outs[k].dtype)
                    start += rows
            total = ins[-2][k].astype(f32) + ins[-1][k].astype(f32)
            outs[k][start:] = total.astype(outs[k].dtype)

    return call(
        kernel,
        [z, c],
        (1,),
        [whole(v.shape) for v in args],
        [whole(shape)] * 4,
        [jax.ShapeDtypeStruct(shape, bf16 if k else f32) for k in range(4)],
        [],
        0,
        *args,
    )


def split(value):
    high = value.astype(bf16)
    return high, (value - high.astype(f32)).astype(bf16)


def basis_parts(left_basis, right_basis):
    def kernel(_, left_ref, right_ref, rounded_ref, left_high, left_low, right_high, right_low):
        rounded_ref[...] = left_ref[...].astype(bf16)
        left_high[...], left_low[...] = split(left_ref[...].T)
        right_high[...], right_low[...] = split(right_ref[...])

    shape = left_basis.shape
    out = jax.ShapeDtypeStruct(shape, bf16)
    return call(kernel, [0], (1,), [whole(shape)] * 2, [whole(shape)] * 5, [out] * 5, [], 0, left_basis, right_basis)


def rotated_step(weight_grad, bases, first_moment, second_moment):
    size = weight_grad.shape[0]
    parts = 3 if size % 384 == 0 else 1
    cut = size // parts

    def fine(a, b):
        return matmul(a[0], b[0]) + (matmul(a[0], b[1]) + matmul(a[1], b[0]))

    def kernel(_, w_ref, l_ref, th_ref, tl_ref, rh_ref, rl_ref, m_ref, v_ref, *refs):
        first_ref, second_ref, update_ref, high, low = refs
        step = pl.program_id(0)

        @pl.when(step == 0)
        def _():
            turned = fine((th_ref[...], tl_ref[...]), split(w_ref[...]))
            high[...], low[...] = split(turned)

        right = rh_ref[...], rl_ref[...]
        rotated = fine((high[...], low[...]), right)
        new_first = 0.9 * m_ref[...] + 0.1 * rotated
        new_second = 0.95 * v_ref[...] + 0.05 * rotated * rotated
        first_ref[...] = new_first
        second_ref[...] = new_second
        ratio = new_first / (jnp.sqrt(new_second) + 1e-08)
        back = matmul(l_ref[...], ratio.astype(bf16))
        update = matmul(back.astype(bf16), right[0], 1, 1)

        @pl.when(step == 0)
        def _():
            update_ref[...] = update

        @pl.when(step > 0)
        def _():
            update_ref[...] += update

    columns = pl.BlockSpec((size, cut), lambda i, _: (0, i))
    out = jax.ShapeDtypeStruct((size, size), f32)
    return call(
        kernel,
        [0],
        (parts,),
        [whole((size, size))] * 4 + [columns] * 4,
        [columns, columns, whole((size, size))],
        [out] * 3,
        [pltpu.VMEM((size, size), bf16)] * 2,
        16 * size**3,
        weight_grad,
        *bases,
        first_moment,
        second_moment,
    )


def shards(
    tokens, cotangent, w_in, w_out, first_moment, rotated_second_moment, left_basis, right_basis
):
    yl, z, c, x, yh = (lax.axis_index(name) for name in ROW + COL)
    rows, width = tokens.shape
    token_count = 16 * rows
    half, block = token_count // 2, token_count // 8
    grad_scale = token_count ** (-0.5)

    def bf(value):
        return value.astype(bf16)

    def halves(value):
        parts = value.reshape(2, rows // 2, width)
        return [lax.dynamic_index_in_dim(parts, at, 0, False) for at in (yh, 1 - yh)]

    both = lax.all_gather(jnp.stack(halves(tokens) + halves(cotangent)), ROW, axis=1, tiled=True)
    w_in_turned, w_out_turned, bases = lax.optimization_barrier(
        (w_in.T, w_out.T, basis_parts(left_basis, right_basis))
    )

    leaving = bf(matmul(both[3], w_out_turned))
    back_arrived = shift(leaving, "yh", 1)
    leaving, w_in_later = lax.optimization_barrier((leaving, w_in))
    terms = bf(matmul(both[:2].reshape(token_count, width), w_in_later)).reshape(2, half, width)
    forward = lax.psum_scatter(terms, "x", scatter_dimension=1, tiled=True)
    staying = matmul(both[2], w_out_turned)
    line = both[:2].reshape(token_count, width).T
    back_arrived, staying, line = lax.optimization_barrier((back_arrived, staying, line))

    total = bf(add(staying, back_arrived))
    parts = [lax.dynamic_slice_in_dim(total, ((x + k) % 4) * block, block, 0) for k in range(4)]
    back = ring_send(parts, "x")
    parts, forward = lax.optimization_barrier((parts, forward))
    activation, derivative = gelu_pair(add(forward[0], shift(forward[1], "yh", 1)))
    act, derivative, back = lax.optimization_barrier((bf(activation), derivative, back))

    acts = ring_gather(act)
    grad = bf(add(parts[0], *back) * derivative)
    pair = shift(grad, "yh", 1)
    acts, grad, pair = lax.optimization_barrier((acts, grad, pair))

    grads = lax.all_gather(jnp.stack([grad, pair]), "x", axis=1, tiled=True)
    turned = jnp.concatenate([act] + acts + [act] + acts[:2])
    act_own = lax.dynamic_slice_in_dim(turned, ((4 - x) % 4) * block, half, 0)
    act_other = shift(act_own, "yh", 1)
    mixed_own = bf(matmul(act_own, w_out))
    out_grad = matmul(act_own, both[2], 0, 0)
    act_other, mixed_own, out_grad = lax.optimization_barrier((act_other, mixed_own, out_grad))
    mixed = jnp.concatenate([mixed_own, bf(matmul(act_other, w_out))])
    grads, mixed = lax.optimization_barrier((grads, mixed))

    carried = bf(matmul(grads.reshape(token_count, width), w_in_turned))
    terms = jnp.concatenate([mixed, carried]).reshape(8, half // 2, width)
    sums = lax.psum_scatter(terms, ("z", "c"), scatter_dimension=1, tiled=True)
    terms, grads = lax.optimization_barrier((terms, grads))
    weight_grad = grad_scale * (matmul(line[:, :half], grads[0]) + matmul(line[:, half:], grads[1]))
    left_send, left_keep, *right = gram_terms(weight_grad, z, c, x, yh)
    left_arrived = shift(left_send, "c", 1)
    left_arrived, right, weight_grad = lax.optimization_barrier((left_arrived, right, weight_grad))
    chip = core_sums(z, c, [], (left_keep, left_arrived))
    chip_arrived = ring_send(chip, "z")
    right_arrived = ring_send(right, "x")
    new_first, new_second, update = rotated_step(weight_grad, bases, first_moment, rotated_second_moment)
    chip, chip_arrived, right_arrived, update, act_other = lax.optimization_barrier(
        (chip, chip_arrived, right_arrived, update, act_other)
    )

    right_own = add(*[v[0] for v in (right[0], *right_arrived)])
    right_other = bf(add(*[v[1] for v in (right[0], *right_arrived)]))
    right_stat = add(right_own, shift(right_other, "yh", 1))
    out_grad = bf(grad_scale * (out_grad + matmul(act_other, both[3], 0, 0)))
    left = add(chip[0], *chip_arrived).reshape(2, -1, width)

    def along_yl(value, axis):
        mine, theirs = (lax.dynamic_index_in_dim(value, at, axis, False) for at in (yl, 1 - yl))
        return mine.reshape(-1, width), bf(theirs.reshape(-1, width))

    left_mine, left_theirs = along_yl(left, 0)
    left_stat = add(left_mine, shift(left_theirs, "yl", 1))
    mine, theirs = along_yl(sums.reshape(4, 2, rows // 2, width), 1)
    last = bf(add(mine, shift(theirs, "yl", 1)))
    mixed, carried = last[:rows], last[rows:]

    def ordered(value):
        own, other = value[: rows // 2], value[rows // 2 :]
        return jnp.concatenate([jnp.where(yh == 0, own, other), jnp.where(yh == 0, other, own)])

    layer_out, input_grad = ordered(mixed), ordered(carried)
    return (layer_out, input_grad, out_grad, update, new_first, new_second, left_stat, right_stat)


def solution(mesh):
    fine = Mesh(mesh.devices.reshape(2, 4, 2, 4, 2), ROW + COL)
    in_specs = (
        P(ROW, COL),
        P(ROW, COL),
        P(COL, ROW),
        P(ROW, COL),
        P(COL, ROW),
        P(COL, ROW),
        P(COL, None),
        P(ROW, None),
    )
    out_specs = (
        P(ROW, COL),
        P(ROW, COL),
        P(ROW, COL),
        P(COL, ROW),
        P(COL, ROW),
        P(COL, ROW),
        P(COL + ROW, None),
        P(ROW + COL, None),
    )
    return jax.shard_map(shards, mesh=fine, in_specs=in_specs, out_specs=out_specs, check_vma=False)
```

```python
import jax
import jax.numpy as jnp
from jax import lax
from jax.experimental import pallas as pl
from jax.experimental.pallas import tpu as pltpu
from jax.sharding import Mesh, PartitionSpec as P

D = 6144
HID = 12288

bf16 = jnp.bfloat16
f32 = jnp.float32

ROW = ("yl", "z", "c")
COL = ("x", "yh")
SIZES = {"yl": 2, "z": 4, "c": 2, "x": 4, "yh": 2}


def gelu_pair(hidden):
    normal_cdf = 0.5 * (1.0 + jax.scipy.special.erf(hidden * 0.7071067811865476))
    activation = hidden * normal_cdf
    derivative = normal_cdf + hidden * jnp.exp(-0.5 * hidden * hidden) * 0.3989422804014327
    return (activation, derivative)


def shift(value, axis, by):
    size = SIZES[axis]
    return lax.ppermute(value, axis, [(i, (i + by) % size) for i in range(size)])


def add(*terms):
    total = terms[0].astype(f32)
    for term in terms[1:]:
        total = total + term.astype(f32)
    return total


def matmul(a, b, ca=1, cb=0):
    return lax.dot_general(a, b, (((ca,), (cb,)), ((), ())), preferred_element_type=f32)


def ring_send(parts, ring):
    return [shift(parts[k].astype(bf16), ring, k) for k in (2, 1, 3)]


def ring_gather(block):
    return [shift(block, "x", -k) for k in (1, 2, 3)]


def whole(shape):
    return pl.BlockSpec(shape, lambda *_: (0,) * len(shape))


def call(kernel, scalars, grid, in_specs, out_specs, out_shape, scratch, flops, *args):
    moved = sum(v.size * v.dtype.itemsize for v in args) + sum(
        v.size * jnp.dtype(v.dtype).itemsize for v in jax.tree.leaves(out_shape)
    )
    return pl.pallas_call(
        kernel,
        out_shape=out_shape,
        grid_spec=pltpu.PrefetchScalarGridSpec(
            num_scalar_prefetch=1,
            grid=grid,
            in_specs=in_specs,
            out_specs=out_specs,
            scratch_shapes=scratch,
        ),
        compiler_params=pltpu.CompilerParams(vmem_limit_bytes=50 * 2**20),
        cost_estimate=pl.CostEstimate(flops=flops, bytes_accessed=moved, transcendentals=0),
    )(jnp.stack([jnp.asarray(v, jnp.int32) for v in scalars]), *args)


def gram_terms(weight_grad, z, c, x, yh):
    size = weight_grad.shape[0]
    left_rows, right_rows = size // 16, size // 8

    def kernel(at, weight_ref, *refs):
        send_ref, keep_ref = refs[:2]
        right_refs, (left, right) = refs[2:6], refs[6:]
        weight = weight_ref[...]
        here, turned = weight.astype(bf16), weight.T.astype(bf16)
        left[...] = (matmul(here, turned) * (1.0 / HID)).reshape(16, left_rows, size)
        right[...] = (matmul(turned, here) * (1.0 / D)).reshape(8, right_rows, size)
        for k in range(4):
            along_z, along_x = lax.rem(at[0] + k, 4), lax.rem(at[2] + k, 4)
            for y in range(2):
                row = y * 8 + along_z * 2
                send_ref[k, y] = left[row + 1 - at[1]].astype(bf16)
                keep_ref[k, y] = left[row + at[1]].astype(bf16)
                other = at[3] if y == 0 else 1 - at[3]
                right_refs[k][y] = right[along_x * 2 + other].astype(bf16)

    shapes = [(4, 2, left_rows, size)] * 2 + [(2, right_rows, size)] * 4
    return call(
        kernel,
        [z, c, x, yh],
        (1,),
        [whole((size, size))],
        [whole(v) for v in shapes],
        [jax.ShapeDtypeStruct(v, bf16) for v in shapes],
        [
            pltpu.VMEM((16, left_rows, size), f32),
            pltpu.VMEM((8, right_rows, size), f32),
        ],
        4 * size**3,
        weight_grad,
    )


def core_sums(z, c, tokens, left):
    width = left[0].shape[-1]
    left = [v.reshape(4, -1, width) for v in left]
    rows = tokens[0][1].shape[2] if tokens else 0
    shape = (2 * len(tokens) * rows + left[0].shape[1], width)
    args = [v for pair in tokens for v in pair] + left

    def kernel(at, *refs):
        ins, outs = refs[: len(args)], refs[len(args) :]
        for k in range(4):
            place = lax.rem(at[0] + k, 4)
            start = 0
            for i in range(len(tokens)):
                for y in range(2):
                    total = ins[2 * i][y, place, at[1]].astype(f32) + ins[2 * i + 1][y, place].astype(f32)
                    outs[k][start : start + rows] = total.astype(outs[k].dtype)
                    start += rows
            total = ins[-2][k].astype(f32) + ins[-1][k].astype(f32)
            outs[k][start:] = total.astype(outs[k].dtype)

    return call(
        kernel,
        [z, c],
        (1,),
        [whole(v.shape) for v in args],
        [whole(shape)] * 4,
        [jax.ShapeDtypeStruct(shape, bf16 if k else f32) for k in range(4)],
        [],
        0,
        *args,
    )


def split(value):
    high = value.astype(bf16)
    return high, (value - high.astype(f32)).astype(bf16)


def basis_parts(left_basis, right_basis):
    def kernel(_, left_ref, right_ref, rounded_ref, left_high, left_low, right_high, right_low):
        rounded_ref[...] = left_ref[...].astype(bf16)
        left_high[...], left_low[...] = split(left_ref[...].T)
        right_high[...], right_low[...] = split(right_ref[...])

    shape = left_basis.shape
    out = jax.ShapeDtypeStruct(shape, bf16)
    return call(kernel, [0], (1,), [whole(shape)] * 2, [whole(shape)] * 5, [out] * 5, [], 0, left_basis, right_basis)


def rotated_step(weight_grad, left, right, first_moment, second_moment):
    size = weight_grad.shape[0]
    parts = 3 if size % 384 == 0 else 1
    cut = size // parts

    def fine(a, b):
        return matmul(a[0], b[0]) + (matmul(a[0], b[1]) + matmul(a[1], b[0]))

    def kernel(_, w_ref, th_ref, tl_ref, rh_ref, rl_ref, m_ref, v_ref, *refs):
        first_ref, second_ref, ratio_ref, high, low = refs
        step = pl.program_id(0)

        @pl.when(step == 0)
        def _():
            turned = fine((th_ref[...], tl_ref[...]), split(w_ref[...]))
            high[...], low[...] = split(turned)

        rotated = fine((high[...], low[...]), (rh_ref[...], rl_ref[...]))
        new_first = 0.9 * m_ref[...] + 0.1 * rotated
        new_second = 0.95 * v_ref[...] + 0.05 * rotated * rotated
        first_ref[...] = new_first
        second_ref[...] = new_second
        ratio_ref[...] = (new_first / (jnp.sqrt(new_second) + 1e-08)).astype(bf16)

    columns = pl.BlockSpec((size, cut), lambda i, _: (0, i))
    out = [jax.ShapeDtypeStruct((size, size), dtype) for dtype in (f32, f32, bf16)]
    return call(
        kernel,
        [0],
        (parts,),
        [whole((size, size))] * 3 + [columns] * 4,
        [columns] * 3,
        out,
        [pltpu.VMEM((size, size), bf16)] * 2,
        12 * size**3,
        weight_grad,
        *left,
        *right,
        first_moment,
        second_moment,
    )


def shards(
    tokens, cotangent, w_in, w_out, first_moment, rotated_second_moment, left_basis, right_basis
):
    yl, z, c, x, yh = (lax.axis_index(name) for name in ROW + COL)
    rows, width = tokens.shape
    token_count = 16 * rows
    half, block = token_count // 2, token_count // 8
    grad_scale = token_count ** (-0.5)

    def bf(value):
        return value.astype(bf16)

    def halves(value):
        parts = value.reshape(2, rows // 2, width)
        return [lax.dynamic_index_in_dim(parts, at, 0, False) for at in (yh, 1 - yh)]

    both = lax.all_gather(jnp.stack(halves(tokens) + halves(cotangent)), ROW, axis=1, tiled=True)
    w_in_turned, w_out_turned, bases = lax.optimization_barrier(
        (w_in.T, w_out.T, basis_parts(left_basis, right_basis))
    )

    leaving = bf(matmul(both[3], w_out_turned))
    back_arrived = shift(leaving, "yh", 1)
    leaving, w_in_later = lax.optimization_barrier((leaving, w_in))
    terms = bf(matmul(both[:2].reshape(token_count, width), w_in_later)).reshape(2, half, width)
    forward = lax.psum_scatter(terms, "x", scatter_dimension=1, tiled=True)
    staying = matmul(both[2], w_out_turned)
    line = both[:2].reshape(token_count, width).T
    back_arrived, staying, line = lax.optimization_barrier((back_arrived, staying, line))

    total = bf(add(staying, back_arrived))
    parts = [lax.dynamic_slice_in_dim(total, ((x + k) % 4) * block, block, 0) for k in range(4)]
    back = ring_send(parts, "x")
    parts, forward = lax.optimization_barrier((parts, forward))
    activation, derivative = gelu_pair(add(forward[0], shift(forward[1], "yh", 1)))
    act, derivative, back = lax.optimization_barrier((bf(activation), derivative, back))

    acts = ring_gather(act)
    grad = bf(add(parts[0], *back) * derivative)
    pair = shift(grad, "yh", 1)
    act_own = jnp.zeros((half, width), bf16)
    for k, piece in ((0, act), (1, acts[0]), (3, acts[2]), (2, acts[1])):
        act_own = lax.dynamic_update_slice_in_dim(act_own, piece, ((x + k) % 4) * block, 0)
    act_own, grad, pair = lax.optimization_barrier((act_own, grad, pair))

    grads = lax.all_gather(jnp.stack([grad, pair]), "x", axis=1, tiled=True)
    act_other = shift(act_own, "yh", 1)
    mixed_own = bf(matmul(act_own, w_out))
    out_grad = matmul(act_own, both[2], 0, 0)
    act_other, mixed_own, out_grad = lax.optimization_barrier((act_other, mixed_own, out_grad))
    mixed_other = bf(matmul(act_other, w_out))
    grads, mixed_other = lax.optimization_barrier((grads, mixed_other))

    carried = bf(matmul(grads.reshape(token_count, width), w_in_turned))
    terms = jnp.concatenate([mixed_own, mixed_other, carried]).reshape(8, half // 2, width)
    sums = lax.psum_scatter(terms, ("z", "c"), scatter_dimension=1, tiled=True)
    terms, grads = lax.optimization_barrier((terms, grads))
    weight_grad = grad_scale * (matmul(line[:, :half], grads[0]) + matmul(line[:, half:], grads[1]))
    left_send, left_keep, *right = gram_terms(weight_grad, z, c, x, yh)
    left_arrived = shift(left_send, "c", 1)
    left_arrived, right, weight_grad = lax.optimization_barrier((left_arrived, right, weight_grad))
    chip = core_sums(z, c, [], (left_keep, left_arrived))
    right_arrived = ring_send(right, "x")
    new_first, new_second, ratio = rotated_step(
        weight_grad, bases[1:3], bases[3:], first_moment, rotated_second_moment
    )
    chip, right, right_arrived, ratio = lax.optimization_barrier((chip, right, right_arrived, ratio))

    def along_yl(value, axis):
        mine, theirs = (lax.dynamic_index_in_dim(value, at, axis, False) for at in (yl, 1 - yl))
        return mine.reshape(-1, width), bf(theirs.reshape(-1, width))

    right_own = add(*[v[0] for v in (right[0], *right_arrived)])
    right_other = bf(add(*[v[1] for v in (right[0], *right_arrived)]))
    right_stat = add(right_own, shift(right_other, "yh", 1))
    right_stat, ratio, act_other, chip, sums = lax.optimization_barrier((right_stat, ratio, act_other, chip, sums))

    mine, theirs = along_yl(sums.reshape(4, 2, rows // 2, width), 1)
    arrived = shift(theirs, "yl", 1)
    chip_arrived = ring_send(chip, "z")
    update = matmul(bf(matmul(bases[0], ratio)), bases[3], 1, 1)
    chip_arrived, update, chip, act_other = lax.optimization_barrier((chip_arrived, update, chip, act_other))
    left = add(chip[0], *chip_arrived).reshape(2, -1, width)
    left_mine, left_theirs = along_yl(left, 0)
    left_stat = add(left_mine, shift(left_theirs, "yl", 1))
    out_grad = bf(grad_scale * (out_grad + matmul(act_other, both[3], 0, 0)))
    last = bf(add(mine, arrived))
    mixed, carried = last[:rows], last[rows:]

    def ordered(value):
        own, other = value[: rows // 2], value[rows // 2 :]
        return jnp.concatenate([jnp.where(yh == 0, own, other), jnp.where(yh == 0, other, own)])

    layer_out, input_grad = ordered(mixed), ordered(carried)
    return (layer_out, input_grad, out_grad, update, new_first, new_second, left_stat, right_stat)


def solution(mesh):
    fine = Mesh(mesh.devices.reshape(2, 4, 2, 4, 2), ROW + COL)
    in_specs = (
        P(ROW, COL),
        P(ROW, COL),
        P(COL, ROW),
        P(ROW, COL),
        P(COL, ROW),
        P(COL, ROW),
        P(COL, None),
        P(ROW, None),
    )
    out_specs = (
        P(ROW, COL),
        P(ROW, COL),
        P(ROW, COL),
        P(COL, ROW),
        P(COL, ROW),
        P(COL, ROW),
        P(COL + ROW, None),
        P(ROW + COL, None),
    )
    return jax.shard_map(shards, mesh=fine, in_specs=in_specs, out_specs=out_specs, check_vma=False)
```

```python
import jax
import jax.numpy as jnp
from jax import lax
from jax.experimental import pallas as pl
from jax.experimental.pallas import tpu as pltpu
from jax.sharding import Mesh, PartitionSpec as P

D = 6144
HID = 12288

bf16 = jnp.bfloat16
f32 = jnp.float32

ROW = ("yl", "z", "c")
COL = ("x", "yh")
SIZES = {"yl": 2, "z": 4, "c": 2, "x": 4, "yh": 2}


def gelu_pair(hidden):
    normal_cdf = 0.5 * (1.0 + jax.scipy.special.erf(hidden * 0.7071067811865476))
    activation = hidden * normal_cdf
    derivative = normal_cdf + hidden * jnp.exp(-0.5 * hidden * hidden) * 0.3989422804014327
    return (activation, derivative)


def shift(value, axis, by):
    size = SIZES[axis]
    return lax.ppermute(value, axis, [(i, (i + by) % size) for i in range(size)])


def add(*terms):
    total = terms[0].astype(f32)
    for term in terms[1:]:
        total = total + term.astype(f32)
    return total


def matmul(a, b, ca=1, cb=0):
    return lax.dot_general(a, b, (((ca,), (cb,)), ((), ())), preferred_element_type=f32)


def ring_send(parts, ring):
    return [shift(parts[k].astype(bf16), ring, k) for k in (2, 1, 3)]


def ring_gather(block):
    return [shift(block, "x", -k) for k in (1, 2, 3)]


def whole(shape):
    return pl.BlockSpec(shape, lambda *_: (0,) * len(shape))


def call(kernel, scalars, grid, in_specs, out_specs, out_shape, scratch, flops, *args):
    moved = sum(v.size * v.dtype.itemsize for v in args) + sum(
        v.size * jnp.dtype(v.dtype).itemsize for v in jax.tree.leaves(out_shape)
    )
    return pl.pallas_call(
        kernel,
        out_shape=out_shape,
        grid_spec=pltpu.PrefetchScalarGridSpec(
            num_scalar_prefetch=1,
            grid=grid,
            in_specs=in_specs,
            out_specs=out_specs,
            scratch_shapes=scratch,
        ),
        compiler_params=pltpu.CompilerParams(vmem_limit_bytes=50 * 2**20),
        cost_estimate=pl.CostEstimate(flops=flops, bytes_accessed=moved, transcendentals=0),
    )(jnp.stack([jnp.asarray(v, jnp.int32) for v in scalars]), *args)


def gram_terms(weight_grad, z, c, x, yh):
    size = weight_grad.shape[0]
    left_rows, right_rows = size // 16, size // 8

    def kernel(at, weight_ref, *refs):
        send_ref, keep_ref = refs[:2]
        right_refs, (left, right) = refs[2:6], refs[6:]
        weight = weight_ref[...]
        here, turned = weight.astype(bf16), weight.T.astype(bf16)
        left[...] = (matmul(here, turned) * (1.0 / HID)).reshape(16, left_rows, size)
        right[...] = (matmul(turned, here) * (1.0 / D)).reshape(8, right_rows, size)
        for k in range(4):
            along_z, along_x = lax.rem(at[0] + k, 4), lax.rem(at[2] + k, 4)
            for y in range(2):
                row = y * 8 + along_z * 2
                send_ref[k, y] = left[row + 1 - at[1]].astype(bf16)
                keep_ref[k, y] = left[row + at[1]].astype(bf16)
                other = at[3] if y == 0 else 1 - at[3]
                right_refs[k][y] = right[along_x * 2 + other].astype(bf16)

    shapes = [(4, 2, left_rows, size)] * 2 + [(2, right_rows, size)] * 4
    return call(
        kernel,
        [z, c, x, yh],
        (1,),
        [whole((size, size))],
        [whole(v) for v in shapes],
        [jax.ShapeDtypeStruct(v, bf16) for v in shapes],
        [
            pltpu.VMEM((16, left_rows, size), f32),
            pltpu.VMEM((8, right_rows, size), f32),
        ],
        4 * size**3,
        weight_grad,
    )


def core_sums(z, c, tokens, left):
    width = left[0].shape[-1]
    left = [v.reshape(4, -1, width) for v in left]
    rows = tokens[0][1].shape[2] if tokens else 0
    shape = (2 * len(tokens) * rows + left[0].shape[1], width)
    args = [v for pair in tokens for v in pair] + left

    def kernel(at, *refs):
        ins, outs = refs[: len(args)], refs[len(args) :]
        for k in range(4):
            place = lax.rem(at[0] + k, 4)
            start = 0
            for i in range(len(tokens)):
                for y in range(2):
                    total = ins[2 * i][y, place, at[1]].astype(f32) + ins[2 * i + 1][y, place].astype(f32)
                    outs[k][start : start + rows] = total.astype(outs[k].dtype)
                    start += rows
            total = ins[-2][k].astype(f32) + ins[-1][k].astype(f32)
            outs[k][start:] = total.astype(outs[k].dtype)

    return call(
        kernel,
        [z, c],
        (1,),
        [whole(v.shape) for v in args],
        [whole(shape)] * 4,
        [jax.ShapeDtypeStruct(shape, bf16 if k else f32) for k in range(4)],
        [],
        0,
        *args,
    )


def split(value):
    high = value.astype(bf16)
    return high, (value - high.astype(f32)).astype(bf16)


def basis_parts(left_basis, right_basis):
    def kernel(_, left_ref, right_ref, rounded_ref, left_high, left_low, right_high, right_low):
        rounded_ref[...] = left_ref[...].astype(bf16)
        left_high[...], left_low[...] = split(left_ref[...].T)
        right_high[...], right_low[...] = split(right_ref[...])

    shape = left_basis.shape
    out = jax.ShapeDtypeStruct(shape, bf16)
    return call(kernel, [0], (1,), [whole(shape)] * 2, [whole(shape)] * 5, [out] * 5, [], 0, left_basis, right_basis)


def rotated_step(weight_grad, left, right, first_moment, second_moment):
    size = weight_grad.shape[0]
    parts = 3 if size % 384 == 0 else 1
    cut = size // parts

    def fine(a, b):
        return matmul(a[0], b[0]) + (matmul(a[0], b[1]) + matmul(a[1], b[0]))

    def kernel(_, w_ref, th_ref, tl_ref, rh_ref, rl_ref, m_ref, v_ref, *refs):
        first_ref, second_ref, ratio_ref, high, low = refs
        step = pl.program_id(0)

        @pl.when(step == 0)
        def _():
            turned = fine((th_ref[...], tl_ref[...]), split(w_ref[...]))
            high[...], low[...] = split(turned)

        rotated = fine((high[...], low[...]), (rh_ref[...], rl_ref[...]))
        new_first = 0.9 * m_ref[...] + 0.1 * rotated
        new_second = 0.95 * v_ref[...] + 0.05 * rotated * rotated
        first_ref[...] = new_first
        second_ref[...] = new_second
        ratio_ref[...] = (new_first / (jnp.sqrt(new_second) + 1e-08)).astype(bf16)

    columns = pl.BlockSpec((size, cut), lambda i, _: (0, i))
    out = [jax.ShapeDtypeStruct((size, size), dtype) for dtype in (f32, f32, bf16)]
    return call(
        kernel,
        [0],
        (parts,),
        [whole((size, size))] * 3 + [columns] * 4,
        [columns] * 3,
        out,
        [pltpu.VMEM((size, size), bf16)] * 2,
        12 * size**3,
        weight_grad,
        *left,
        *right,
        first_moment,
        second_moment,
    )


def shards(
    tokens, cotangent, w_in, w_out, first_moment, rotated_second_moment, left_basis, right_basis
):
    yl, z, c, x, yh = (lax.axis_index(name) for name in ROW + COL)
    rows, width = tokens.shape
    token_count = 16 * rows
    half, block = token_count // 2, token_count // 8
    grad_scale = token_count ** (-0.5)

    def bf(value):
        return value.astype(bf16)

    def halves(value):
        parts = value.reshape(2, rows // 2, width)
        return [lax.dynamic_index_in_dim(parts, at, 0, False) for at in (yh, 1 - yh)]

    both = lax.all_gather(jnp.stack(halves(tokens) + halves(cotangent)), ROW, axis=1, tiled=True)
    w_in, w_out, bases = lax.optimization_barrier((w_in, w_out, basis_parts(left_basis, right_basis)))

    leaving = bf(matmul(both[3], w_out, 1, 1))
    back_arrived = shift(leaving, "yh", 1)
    leaving, w_in_later = lax.optimization_barrier((leaving, w_in))
    terms = bf(matmul(both[:2].reshape(token_count, width), w_in_later)).reshape(2, half, width)
    forward = lax.psum_scatter(terms, "x", scatter_dimension=1, tiled=True)
    staying = matmul(both[2], w_out, 1, 1)
    line = both[:2].reshape(token_count, width).T
    back_arrived, staying, line = lax.optimization_barrier((back_arrived, staying, line))

    total = bf(add(staying, back_arrived))
    parts = [lax.dynamic_slice_in_dim(total, ((x + k) % 4) * block, block, 0) for k in range(4)]
    back = ring_send(parts, "x")
    parts, forward = lax.optimization_barrier((parts, forward))
    activation, derivative = gelu_pair(add(forward[0], shift(forward[1], "yh", 1)))
    act, derivative, back = lax.optimization_barrier((bf(activation), derivative, back))

    acts = ring_gather(act)
    grad = bf(add(parts[0], *back) * derivative)
    pair = shift(grad, "yh", 1)
    act_own = jnp.zeros((half, width), bf16)
    for k, piece in ((0, act), (1, acts[0]), (3, acts[2]), (2, acts[1])):
        act_own = lax.dynamic_update_slice_in_dim(act_own, piece, ((x + k) % 4) * block, 0)
    act_own, grad, pair = lax.optimization_barrier((act_own, grad, pair))

    grads = lax.all_gather(jnp.stack([grad, pair]), "x", axis=1, tiled=True)
    act_other = shift(act_own, "yh", 1)
    mixed_own = bf(matmul(act_own, w_out))
    out_grad = matmul(act_own, both[2], 0, 0)
    act_other, mixed_own, out_grad = lax.optimization_barrier((act_other, mixed_own, out_grad))
    mixed_other = bf(matmul(act_other, w_out))
    grads, mixed_other = lax.optimization_barrier((grads, mixed_other))

    carried = bf(matmul(grads.reshape(token_count, width), w_in, 1, 1))
    terms = jnp.concatenate([mixed_own, mixed_other, carried]).reshape(8, half // 2, width)
    sums = lax.psum_scatter(terms, ("z", "c"), scatter_dimension=1, tiled=True)
    terms, grads = lax.optimization_barrier((terms, grads))
    weight_grad = grad_scale * (matmul(line[:, :half], grads[0]) + matmul(line[:, half:], grads[1]))
    left_send, left_keep, *right = gram_terms(weight_grad, z, c, x, yh)
    left_arrived = shift(left_send, "c", 1)
    left_arrived, right, weight_grad = lax.optimization_barrier((left_arrived, right, weight_grad))
    chip = core_sums(z, c, [], (left_keep, left_arrived))
    right_arrived = ring_send(right, "x")
    new_first, new_second, ratio = rotated_step(
        weight_grad, bases[1:3], bases[3:], first_moment, rotated_second_moment
    )
    chip, right, right_arrived, ratio = lax.optimization_barrier((chip, right, right_arrived, ratio))

    def along_yl(value, axis):
        mine, theirs = (lax.dynamic_index_in_dim(value, at, axis, False) for at in (yl, 1 - yl))
        return mine.reshape(-1, width), bf(theirs.reshape(-1, width))

    right_own = add(*[v[0] for v in (right[0], *right_arrived)])
    right_other = bf(add(*[v[1] for v in (right[0], *right_arrived)]))
    right_stat = add(right_own, shift(right_other, "yh", 1))
    right_stat, ratio, act_other, chip, sums = lax.optimization_barrier((right_stat, ratio, act_other, chip, sums))

    mine, theirs = along_yl(sums.reshape(4, 2, rows // 2, width), 1)
    arrived = shift(theirs, "yl", 1)
    chip_arrived = ring_send(chip, "z")
    update = matmul(bf(matmul(bases[0], ratio)), bases[3], 1, 1)
    chip_arrived, update, chip, act_other = lax.optimization_barrier((chip_arrived, update, chip, act_other))
    left = add(chip[0], *chip_arrived).reshape(2, -1, width)
    left_mine, left_theirs = along_yl(left, 0)
    left_stat = add(left_mine, shift(left_theirs, "yl", 1))
    out_grad = bf(grad_scale * (out_grad + matmul(act_other, both[3], 0, 0)))
    last = bf(add(mine, arrived))
    mixed, carried = last[:rows], last[rows:]

    def ordered(value):
        own, other = value[: rows // 2], value[rows // 2 :]
        return jnp.concatenate([jnp.where(yh == 0, own, other), jnp.where(yh == 0, other, own)])

    layer_out, input_grad = ordered(mixed), ordered(carried)
    return (layer_out, input_grad, out_grad, update, new_first, new_second, left_stat, right_stat)


def solution(mesh):
    fine = Mesh(mesh.devices.reshape(2, 4, 2, 4, 2), ROW + COL)
    in_specs = (
        P(ROW, COL),
        P(ROW, COL),
        P(COL, ROW),
        P(ROW, COL),
        P(COL, ROW),
        P(COL, ROW),
        P(COL, None),
        P(ROW, None),
    )
    out_specs = (
        P(ROW, COL),
        P(ROW, COL),
        P(ROW, COL),
        P(COL, ROW),
        P(COL, ROW),
        P(COL, ROW),
        P(COL + ROW, None),
        P(ROW + COL, None),
    )
    return jax.shard_map(shards, mesh=fine, in_specs=in_specs, out_specs=out_specs, check_vma=False)
```
